32 devices in a mesh: row: 8 (over z, y), col: 4 (over x, core).
Axes of the slice: x: 2, y: 2, z: 4, core: 2. Of those that a mesh axis runs over, the one named last changes fastest.
Arguments:
- leaf_grad: bfloat16 [32, 32, 1024], P('row', None, 'col'), may hold values from -6 to 6
- leaf_inv: bfloat16 [32, 1024, 1024], P('row', 'col'), as said below
- leaf_cpl: bfloat16 [32, 1024, 512], P('row', 'col'), may hold values from -0.125 to 0.125
- leaf_size: int32 [32], P('row'), may hold values from 256 to 1024, as said below
- leaf_parent: int32 [32], P('row'), may hold values from 0 to 3
- leaf_map: int32 [32, 512], P('row'), may hold values from 0 to 2047
- mid_grad: bfloat16 [32, 4, 2048], P(None, 'col', 'row'), may hold values from -6 to 6
- mid_inv: bfloat16 [4, 2048, 2048], P('col', 'row'), as said below
- mid_cpl: bfloat16 [4, 2048, 512], P('col', 'row'), may hold values from -0.125 to 0.125
- mid_map: int32 [4, 512], replicated, may hold values from 0 to 2047
- root_grad: bfloat16 [32, 2048], P(None, 'row'), may hold values from -6 to 6
- root_inv: bfloat16 [2048, 2048], P('row'), as said below
Outputs:
- leaf_x: float32 [32, 32, 1024], P('row', None, 'col')
- mid_x: float32 [32, 4, 2048], P(None, 'col', 'row')
- root_x: float32 [32, 2048], P(None, 'row')
The draws below stay inside these ranges and needn't reach their ends.
Inputs may be any that keep to these rules, and one draw needn't show every extreme that they name: `leaf_size`: some leaf in every draw has 1024 live pivot columns. `leaf_map`: columns may repeat. `mid_map`: columns may repeat. `leaf_inv`: upper triangular; diagonal entries between 1 and 1.25, entries above the diagonal of scale 1024 ** -0.5. `mid_inv`: each front's block is upper triangular; diagonal entries between 1 and 1.25, entries above the diagonal of scale 2048 ** -0.5. `root_inv`: upper triangular; diagonal entries between 1 and 1.25, entries above the diagonal of scale 2048 ** -0.5.
All inputs are finite; a program needn't handle non-finite values.
Results may differ from the reference program's by a relative error of at most 0.012.
Values may be sent and summed in bfloat16 or wider, within the bound.
A program may use at most 64 MiB of HBM per device.

```python
import math
import jax
import jax.numpy as jnp
from jax import lax

K = 32
P0 = 1024
C0 = 512
P1 = 2048
C1 = 512
P2 = 2048
LEAF_DEV = 4
NLEAF = 32
N_MID = 4
N_ROW = 8
N_COL = 4


def triangle_stack(key, count, order):
    upper_vals = jax.random.normal(key, (count, order, order), jnp.float32)
    diag_vals = 1.0 + 0.25 * jax.random.uniform(jax.random.fold_in(key, 3), (count, order, order), jnp.float32)
    row_ids = lax.broadcasted_iota(jnp.int32, (count, order, order), 1)
    col_ids = lax.broadcasted_iota(jnp.int32, (count, order, order), 2)
    scaled = upper_vals / math.sqrt(order)
    return jnp.where(col_ids > row_ids, scaled, jnp.where(col_ids == row_ids, diag_vals, 0.0))


def draw_leaf_inv(key, part):
    return triangle_stack(key, NLEAF, P0).astype(jnp.bfloat16)


def draw_mid_inv(key, part):
    return triangle_stack(key, N_MID, P1).astype(jnp.bfloat16)


def draw_root_inv(key, part):
    return triangle_stack(key, 1, P2)[0].astype(jnp.bfloat16)


def draw_leaf_size(key, part):
    counts = jax.random.randint(key, (NLEAF,), P0 // 4, P0 + 1)
    chosen = jax.random.randint(jax.random.fold_in(key, 7), (), 0, NLEAF)
    return counts.at[chosen].set(P0).astype(jnp.int32)


def place_ends(values, rng, low, largest):
    extent = values.shape
    spot = [jax.random.randint(jax.random.fold_in(rng, axis), (), 0, extent[axis]) for axis in range(len(extent))]
    values = values.at[tuple(spot)].set(low)
    longest = extent.index(max(extent))
    spot[longest] = (spot[longest] + 1) % extent[longest]
    return values.at[tuple(spot)].set(largest)


def steps_of(stream_key, shape, shards, low, top_value):
    factor_of, own = 1.0, jax.random.fold_in(stream_key, 6)
    for dim, parts in shards:
        draws = jnp.exp(jax.random.uniform(jax.random.fold_in(own, dim), (parts,), jnp.float32, low / len(shards), top_value / len(shards)))
        factor_of = factor_of * jnp.repeat(draws, shape[dim] // parts).reshape([-1 if axis == dim else 1 for axis in range(len(shape))])
    return factor_of


def scatter_about(key, extent, scale, reach, split=(), held_as=jnp.bfloat16):
    factor_of = steps_of(key, extent, split, -0.22, 0.18) if split else 1.0
    values = jax.random.normal(key, extent, jnp.float32) * scale * factor_of
    return jnp.minimum(jnp.maximum(values, -reach), reach).astype(held_as)


def setup_inputs(seed: int = 0) -> dict:
    streams_of = jax.random.split(jax.random.key(seed), 13)
    return {
        "leaf_grad": scatter_about(streams_of[0], (NLEAF, K, P0), 1.0, 6.0, ((0, 8), (2, 4))),
        "leaf_inv": draw_leaf_inv(jax.random.fold_in(streams_of[12], 71), 0),
        "leaf_cpl": scatter_about(streams_of[2], (NLEAF, P0, C0), (P0 * max(1, LEAF_DEV * N_ROW * C0 // (N_COL * P1))) ** -0.5, 0.125, ((0, 8), (1, 4))),
        "leaf_size": draw_leaf_size(jax.random.fold_in(streams_of[12], 71), 0),
        "leaf_parent": place_ends(jax.random.randint(streams_of[4], (NLEAF,), 0, N_MID), jax.random.fold_in(streams_of[4], 1), 0, N_MID - 1).astype(jnp.int32),
        "leaf_map": place_ends(jax.random.randint(streams_of[5], (NLEAF, C0), 0, P1), jax.random.fold_in(streams_of[5], 1), 0, P1 - 1).astype(jnp.int32),
        "mid_grad": scatter_about(streams_of[6], (K, N_MID, P1), 1.0, 6.0, ((1, 4), (2, 8))),
        "mid_inv": draw_mid_inv(jax.random.fold_in(streams_of[12], 71), 0),
        "mid_cpl": scatter_about(streams_of[8], (N_MID, P1, C1), (P1 * max(1, N_MID * C1 // P2)) ** -0.5, 0.125, ((0, 4), (1, 8))),
        "mid_map": place_ends(jax.random.randint(streams_of[9], (N_MID, C1), 0, P2), jax.random.fold_in(streams_of[9], 1), 0, P2 - 1).astype(jnp.int32),
        "root_grad": scatter_about(streams_of[10], (K, P2), 1.0, 6.0, ((1, 8),)),
        "root_inv": draw_root_inv(jax.random.fold_in(streams_of[12], 71), 0),
    }


def rounded(values):
    return lax.optimization_barrier(values.astype(jnp.bfloat16))


def reference(leaf_grad, leaf_inv, leaf_cpl, leaf_size, leaf_parent, leaf_map, mid_grad, mid_inv, mid_cpl, mid_map, root_grad, root_inv):
    front = mid_inv.shape[1]
    nmiddle = mid_map.shape[0]
    columns = jnp.arange(P0)

    def leaf_forward(carry, items):
        grad, inverse, couple, size, parent, cmap = items
        mask = columns[None, :] < size
        solved = jnp.dot(grad.astype(jnp.float32), inverse.astype(jnp.float32), preferred_element_type=jnp.float32)
        solved = jnp.where(mask, solved, 0.0)
        share = jnp.dot(rounded(solved).astype(jnp.float32), couple.astype(jnp.float32), preferred_element_type=jnp.float32)
        carry = carry.at[:, parent * front + cmap].add(share)
        return carry, solved

    start = jnp.zeros((K, nmiddle * front), jnp.float32)
    contrib, leaf_y = lax.scan(leaf_forward, start, (leaf_grad, leaf_inv, leaf_cpl, leaf_size, leaf_parent, leaf_map))
    mid_hb = rounded(mid_grad.astype(jnp.float32) - contrib.reshape(K, nmiddle, front))
    inv_three = mid_inv.astype(jnp.float32)
    cpl_three = mid_cpl.astype(jnp.float32)
    mid_y = jnp.einsum('kpa,pab->kpb', mid_hb.astype(jnp.float32), inv_three)
    mid_u = jnp.einsum('kpa,pac->kpc', rounded(mid_y).astype(jnp.float32), cpl_three)
    root_total = jnp.zeros((K, P2), jnp.float32).at[:, mid_map.reshape(-1)].add(mid_u.reshape(K, nmiddle * C1))
    root_hb = rounded(root_grad.astype(jnp.float32) - root_total)
    root_f = root_inv.astype(jnp.float32)
    root_y = jnp.dot(root_hb.astype(jnp.float32), root_f, preferred_element_type=jnp.float32)
    root_x = jnp.dot(rounded(root_y).astype(jnp.float32), root_f.T, preferred_element_type=jnp.float32)
    root_xb = rounded(root_x).astype(jnp.float32)
    coupled = root_xb[:, mid_map]
    mid_w = mid_y - jnp.einsum('kpc,pbc->kpb', coupled, cpl_three)
    mid_x = jnp.einsum('kpa,pba->kpb', rounded(mid_w).astype(jnp.float32), inv_three)
    mid_xb = rounded(mid_x).astype(jnp.float32).reshape(K, nmiddle * front)

    def leaf_backward(items):
        solved, inverse, couple, size, parent, cmap = items
        mask = columns[None, :] < size
        picked = mid_xb[:, parent * front + cmap]
        resid = solved - jnp.dot(picked, couple.astype(jnp.float32).T, preferred_element_type=jnp.float32)
        resid = jnp.where(mask, resid, 0.0)
        return jnp.dot(rounded(resid).astype(jnp.float32), inverse.astype(jnp.float32).T, preferred_element_type=jnp.float32)

    leaf_x = lax.map(leaf_backward, (leaf_y, leaf_inv, leaf_cpl, leaf_size, leaf_parent, leaf_map))
    return leaf_x, mid_x, root_x
```

```python
import functools

import jax
import jax.numpy as jnp
from jax import lax
from jax.experimental import pallas as pl
from jax.experimental.pallas import tpu as pltpu
from jax.sharding import PartitionSpec as P

MESH = pl.DeviceIdType.MESH
F32 = jnp.float32
BF16 = jnp.bfloat16
LANES = 128


def dot(a, b):
    return jnp.dot(a, b, preferred_element_type=F32)


def dot_t(a, b):
    return lax.dot_general(a, b, (((1,), (1,)), ((), ())), preferred_element_type=F32)


def pack(x):
    return jnp.concatenate(
        [x[:, i : i + LANES] for i in range(0, x.shape[1], LANES)], axis=0
    )


def kernel(
    nrow,
    ncol,
    grad_ref,
    inv_hbm,
    cpl_hbm,
    size_ref,
    parent_ref,
    map_ref,
    mgrad_ref,
    minv_hbm,
    mcpl_hbm,
    mmap_ref,
    rgrad_ref,
    rinv_hbm,
    leaf_out,
    mid_out,
    root_out,
    inv,
    cpl,
    minv,
    mcpl,
    rinv,
    pick,
    mpick,
    leaf_y,
    rgrad,
    s_fwd,
    r_fwd,
    s_cpl,
    r_cpl,
    s_con,
    r_con,
    s_mid,
    r_mid,
    s_root,
    r_root,
    s_ry,
    r_ry,
    s_rg,
    r_rg,
    s_rx,
    r_rx,
    s_mw,
    r_mw,
    s_mx,
    r_mx,
    s_pk,
    r_pk,
    s_lw,
    r_lw,
    load_sem,
    send_sem,
    recv_sem,
):
    ndev = nrow * ncol
    row, col = lax.axis_index("row"), lax.axis_index("col")
    me = row * ncol + col
    nleaf, nrhs, share = grad_ref.shape
    kc = nrhs // ncol
    front = minv.shape[1]
    width = minv.shape[0]
    ccols = cpl.shape[2]
    halves = width // LANES

    loads = [
        pltpu.make_async_copy(src, dst, load_sem.at[i])
        for i, (src, dst) in enumerate(
            [(inv_hbm, inv), (cpl_hbm, cpl), (minv_hbm, minv), (mcpl_hbm, mcpl), (rinv_hbm, rinv)]
        )
    ]
    for load in loads:
        load.start()

    barrier = pltpu.get_barrier_semaphore()

    def greet(t, _):
        other = lax.rem(me + t, ndev)
        pl.semaphore_signal(
            barrier,
            inc=1,
            device_id=(lax.div(other, ncol), lax.rem(other, ncol)),
            device_id_type=MESH,
        )
        return 0

    lax.fori_loop(1, ndev, greet, 0)

    def to_all(phase, src_of, dst):
        def step(t, _):
            other = lax.rem(me + t, ndev)
            orow, ocol = lax.div(other, ncol), lax.rem(other, ncol)
            pltpu.make_async_remote_copy(
                src_ref=src_of(other, ocol),
                dst_ref=dst.at[me],
                send_sem=send_sem.at[phase],
                recv_sem=recv_sem.at[phase],
                device_id=(orow, ocol),
                device_id_type=MESH,
            ).start()
            return 0

        lax.fori_loop(1, ndev, step, 0)

    def to_rows(phase, src_of, dst):
        def step(t, _):
            orow = lax.rem(row + t, nrow)
            pltpu.make_async_remote_copy(
                src_ref=src_of(orow),
                dst_ref=dst.at[row],
                send_sem=send_sem.at[phase],
                recv_sem=recv_sem.at[phase],
                device_id=(orow, col),
                device_id_type=MESH,
            ).start()
            return 0

        lax.fori_loop(1, nrow, step, 0)

    def to_cols(phase, src_of, dst):
        def step(t, _):
            ocol = lax.rem(col + t, ncol)
            pltpu.make_async_remote_copy(
                src_ref=src_of(ocol),
                dst_ref=dst.at[col],
                send_sem=send_sem.at[phase],
                recv_sem=recv_sem.at[phase],
                device_id=(row, ocol),
                device_id_type=MESH,
            ).start()
            return 0

        lax.fori_loop(1, ncol, step, 0)

    def arrive(phase, dst):
        part = dst.at[pl.ds(0, dst.shape[0] - 1)]
        pltpu.make_async_copy(part, part, recv_sem.at[phase]).wait()

    def sent(phase, dst):
        part = dst.at[pl.ds(0, dst.shape[0] - 1)]
        pltpu.make_async_copy(part, part, send_sem.at[phase]).wait()

    def stage_blocks(buf, t):
        for r in range(nrow):
            for c in range(ncol):
                buf[r * ncol + c] = pack(
                    t[c * kc : (c + 1) * kc, r * width : (r + 1) * width]
                ).astype(BF16)

    def unpack_all(buf):
        x = buf[...].astype(F32)
        x = x.reshape(nrow, ncol, halves, kc, LANES)
        return jnp.concatenate(
            [
                x[r, :, h].reshape(ncol * kc, LANES)
                for r in range(nrow)
                for h in range(halves)
            ],
            axis=1,
        ).astype(BF16)

    loads[0].wait()
    for f in range(nleaf):
        part = dot(grad_ref[f], inv[f])
        for c in range(ncol):
            s_fwd[c, f] = part[:, c * share : (c + 1) * share].astype(BF16)
    pl.semaphore_wait(barrier, ndev - 1)
    to_cols(0, lambda c: s_fwd.at[c], r_fwd)
    r_fwd[col] = s_fwd[col]

    step_rows = 256

    def fill(i, _):
        rows = pl.ds(pl.multiple_of(i * step_rows, step_rows), step_rows)
        ids = lax.broadcasted_iota(jnp.int32, (step_rows, ccols), 0) + i * step_rows
        for f in range(nleaf):
            pick[rows, f * ccols : (f + 1) * ccols] = jnp.where(
                ids == map_ref[f : f + 1, :], 1.0, 0.0
            ).astype(BF16)
        return 0

    lax.fori_loop(0, front // step_rows, fill, 0)
    rgrad[...] = rgrad_ref[...].astype(F32)
    loads[1].wait()

    arrive(0, r_fwd)
    firsts = col * share + lax.broadcasted_iota(jnp.int32, (nrhs, share), 1)
    shares = []
    for f in range(nleaf):
        y = r_fwd[0, f].astype(F32)
        for c in range(1, ncol):
            y = y + r_fwd[c, f].astype(F32)
        y = jnp.where(firsts < size_ref[f], y, 0.0)
        leaf_y[f] = y
        shares.append(dot(y.astype(BF16), cpl[f]))
    for c in range(ncol):
        s_cpl[c] = jnp.concatenate(
            [u[c * kc : (c + 1) * kc] for u in shares], axis=0
        ).astype(BF16)
    to_cols(1, lambda c: s_cpl.at[c], r_cpl)
    r_cpl[col] = s_cpl[col]

    def fill_mid(i, _):
        rows = pl.ds(pl.multiple_of(i * step_rows, step_rows), step_rows)
        ids = lax.broadcasted_iota(jnp.int32, (step_rows, ccols), 0) + i * step_rows
        mpick[rows, :] = jnp.where(ids == mmap_ref[pl.ds(col, 1), :], 1.0, 0.0).astype(BF16)
        return 0

    lax.fori_loop(0, front // step_rows, fill_mid, 0)
    loads[2].wait()
    loads[3].wait()
    loads[4].wait()

    arrive(1, r_cpl)
    u = r_cpl[0].astype(F32)
    for c in range(1, ncol):
        u = u + r_cpl[c].astype(F32)
    spread = jnp.concatenate(
        [
            jnp.concatenate(
                [
                    jnp.where(parent_ref[f] == p, u[f * kc : (f + 1) * kc], 0.0)
                    for p in range(ncol)
                ],
                axis=0,
            )
            for f in range(nleaf)
        ],
        axis=1,
    ).astype(BF16)
    stage_blocks(s_con, dot_t(spread, pick[...]))
    to_all(2, lambda d, c: s_con.at[d], r_con)
    r_con[me] = s_con[me]

    arrive(2, r_con)
    got = r_con[...].astype(F32).reshape(nrow, ncol, halves, kc, LANES)
    total = got[0]
    for r in range(1, nrow):
        total = total + got[r]
    contrib = jnp.concatenate(
        [total[:, h].reshape(nrhs, LANES) for h in range(halves)], axis=1
    )
    mid_hb = (mgrad_ref[...].astype(F32) - contrib).astype(BF16)
    part = dot(mid_hb, minv[...])
    for r in range(nrow):
        s_mid[r] = part[:, r * width : (r + 1) * width].astype(BF16)
    to_rows(3, lambda r: s_mid.at[r], r_mid)
    r_mid[row] = s_mid[row]
    arrive(3, r_mid)
    mid_y = r_mid[0].astype(F32)
    for r in range(1, nrow):
        mid_y = mid_y + r_mid[r].astype(F32)

    mid_u = dot(mid_y.astype(BF16), mcpl[...])
    stage_blocks(s_root, dot_t(mid_u.astype(BF16), mpick[...]))
    to_all(4, lambda d, c: s_root.at[d], r_root)
    r_root[me] = s_root[me]
    arrive(4, r_root)
    total = jnp.sum(r_root[...].astype(F32), axis=0)
    root_total = jnp.concatenate(
        [total[h * kc : (h + 1) * kc] for h in range(halves)], axis=1
    )
    mine = rgrad[pl.ds(pl.multiple_of(col * kc, kc), kc), :]
    root_hb = (mine - root_total).astype(BF16)
    part = dot(root_hb, rinv[...])
    for r in range(nrow):
        s_ry[r] = pack(part[:, r * width : (r + 1) * width]).astype(BF16)
    to_rows(5, lambda r: s_ry.at[r], r_ry)
    r_ry[row] = s_ry[row]
    arrive(5, r_ry)
    s_rg[...] = jnp.sum(r_ry[...].astype(F32), axis=0).astype(BF16)
    to_rows(6, lambda r: s_rg, r_rg)
    r_rg[row] = s_rg[...]
    arrive(6, r_rg)
    ry = r_rg[...].astype(F32)
    root_yb = jnp.concatenate(
        [ry[r, h * kc : (h + 1) * kc] for r in range(nrow) for h in range(halves)], axis=1
    ).astype(BF16)
    s_rx[...] = pack(dot_t(root_yb, rinv[...])).astype(BF16)
    to_all(7, lambda d, c: s_rx, r_rx)
    r_rx[me] = s_rx[...]
    arrive(7, r_rx)
    root_xb = unpack_all(r_rx)
    own = r_rx[pl.ds(row * ncol, ncol)].astype(F32).reshape(ncol, halves, kc, LANES)
    for h in range(halves):
        root_out[:, h * LANES : (h + 1) * LANES] = own[:, h].reshape(nrhs, LANES)

    coupled = dot(root_xb, mpick[...]).astype(BF16)
    s_mw[...] = (mid_y - dot_t(coupled, mcpl[...])).astype(BF16)
    to_rows(8, lambda r: s_mw, r_mw)
    r_mw[row] = s_mw[...]
    arrive(8, r_mw)
    full_w = jnp.concatenate([r_mw[r] for r in range(nrow)], axis=1)
    mid_x = dot_t(full_w, minv[...])
    mid_out[...] = mid_x
    for c in range(ncol):
        s_mx[c] = pack(mid_x[c * kc : (c + 1) * kc]).astype(BF16)
    to_all(9, lambda d, c: s_mx.at[c], r_mx)
    r_mx[me] = s_mx[col]
    arrive(9, r_mx)

    every = dot(unpack_all(r_mx), pick[...])
    picked = []
    for f in range(nleaf):
        cols = slice(f * ccols, (f + 1) * ccols)
        x = jnp.where(parent_ref[f] == 0, every[0:kc, cols], 0.0)
        for p in range(1, ncol):
            x = jnp.where(parent_ref[f] == p, every[p * kc : (p + 1) * kc, cols], x)
        picked.append(x)
    s_pk[...] = jnp.concatenate(picked, axis=0).astype(BF16)
    to_cols(10, lambda c: s_pk, r_pk)
    r_pk[col] = s_pk[...]
    arrive(10, r_pk)

    got = r_pk[...].astype(F32)
    for f in range(nleaf):
        xb = jnp.concatenate(
            [got[c, f * kc : (f + 1) * kc] for c in range(ncol)], axis=0
        ).astype(BF16)
        w = leaf_y[f] - dot_t(xb, cpl[f])
        s_lw[f] = jnp.where(firsts < size_ref[f], w, 0.0).astype(BF16)
    to_cols(11, lambda c: s_lw, r_lw)
    r_lw[col] = s_lw[...]
    arrive(11, r_lw)
    for f in range(nleaf):
        w = jnp.concatenate([r_lw[c, f] for c in range(ncol)], axis=1)
        leaf_out[f] = dot_t(w, inv[f])

    for phase, buf in enumerate(
        [r_fwd, r_cpl, r_con, r_mid, r_root, r_ry, r_rg, r_rx, r_mw, r_mx, r_pk, r_lw]
    ):
        sent(phase, buf)


def fused(nrow, ncol, *args):
    (leaf_grad, leaf_inv, leaf_cpl, leaf_size, leaf_parent, leaf_map, mid_grad, mid_inv,
     mid_cpl, mid_map, root_grad, root_inv) = args
    nleaf, nrhs, share = leaf_grad.shape
    order = leaf_inv.shape[2]
    ccols = leaf_cpl.shape[2]
    width, front = mid_inv.shape[1:]
    ndev, kc, halves = nrow * ncol, nrhs // ncol, width // LANES
    vmem = pl.BlockSpec(memory_space=pltpu.VMEM)
    smem = pl.BlockSpec(memory_space=pltpu.SMEM)
    anyw = pl.BlockSpec(memory_space=pl.ANY)
    block = (halves * kc, LANES)
    scratch = [
        ((nleaf, share, order), BF16),
        ((nleaf, share, ccols), BF16),
        ((width, front), BF16),
        ((width, mid_cpl.shape[2]), BF16),
        (root_inv.shape, BF16),
        ((front, nleaf * ccols), BF16),
        ((root_inv.shape[1], mid_cpl.shape[2]), BF16),
        ((nleaf, nrhs, share), F32),
        (root_grad.shape, F32),
        ((ncol, nleaf, nrhs, share), BF16),
        ((ncol, nleaf, nrhs, share), BF16),
        ((ncol, nleaf * kc, ccols), BF16),
        ((ncol, nleaf * kc, ccols), BF16),
        ((ndev, *block), BF16),
        ((ndev, *block), BF16),
        ((nrow, nrhs, width), BF16),
        ((nrow, nrhs, width), BF16),
        ((ndev, *block), BF16),
        ((ndev, *block), BF16),
        ((nrow, *block), BF16),
        ((nrow, *block), BF16),
        (block, BF16),
        ((nrow, *block), BF16),
        (block, BF16),
        ((ndev, *block), BF16),
        ((nrhs, width), BF16),
        ((nrow, nrhs, width), BF16),
        ((ncol, *block), BF16),
        ((ndev, *block), BF16),
        ((nleaf * kc, ccols), BF16),
        ((ncol, nleaf * kc, ccols), BF16),
        ((nleaf, nrhs, share), BF16),
        ((ncol, nleaf, nrhs, share), BF16),
    ]
    phases = 12
    leaf_x, mid_x, root_x = pl.pallas_call(
        functools.partial(kernel, nrow, ncol),
        out_shape=(
            jax.ShapeDtypeStruct((nleaf, nrhs, share), F32),
            jax.ShapeDtypeStruct((nrhs, width), F32),
            jax.ShapeDtypeStruct((nrhs, width), F32),
        ),
        in_specs=[vmem, anyw, anyw, smem, smem, vmem, vmem, anyw, anyw, vmem, vmem, anyw],
        out_specs=(vmem, vmem, vmem),
        scratch_shapes=[pltpu.VMEM(shape, dtype) for shape, dtype in scratch]
        + [
            pltpu.SemaphoreType.DMA((5,)),
            pltpu.SemaphoreType.DMA((phases,)),
            pltpu.SemaphoreType.DMA((phases,)),
        ],
        compiler_params=pltpu.CompilerParams(
            collective_id=0, has_side_effects=True, vmem_limit_bytes=48 * 2**20
        ),
    )(
        leaf_grad, leaf_inv, leaf_cpl, leaf_size, leaf_parent, leaf_map, mid_grad[:, 0, :],
        mid_inv[0], mid_cpl[0], mid_map, root_grad, root_inv,
    )
    return leaf_x, mid_x[:, None, :], root_x


def body(
    leaf_grad,
    leaf_inv,
    leaf_cpl,
    leaf_size,
    leaf_parent,
    leaf_map,
    mid_grad,
    mid_inv,
    mid_cpl,
    mid_map,
    root_grad,
    root_inv,
):
    ncolumns = lax.axis_size("col")
    row_id = lax.axis_index("row")
    col_id = lax.axis_index("col")
    nleaves = leaf_inv.shape[0]
    share_rows = leaf_inv.shape[1]
    nrhs = leaf_grad.shape[1]
    front = mid_inv.shape[2]
    mid_rows = mid_inv.shape[1]
    nmiddle = mid_map.shape[0]
    root_order = root_inv.shape[1]
    root_rows = root_inv.shape[0]
    inv_block = mid_inv[0]
    cpl_block = mid_cpl[0]
    first_cols = col_id * share_rows + lax.iota(jnp.int32, share_rows)
    live = (first_cols[None, :] < leaf_size[:, None])[:, None, :]
    partial_value = jnp.einsum(
        "lkp,lpq->lkq", leaf_grad, leaf_inv, preferred_element_type=jnp.float32
    )
    leaf_y = jnp.where(
        live, lax.psum_scatter(partial_value, "col", scatter_dimension=2, tiled=True), 0.0
    )
    leaf_yb = leaf_y.astype(jnp.bfloat16)
    shares = jnp.einsum("lkp,lpc->klc", leaf_yb, leaf_cpl, preferred_element_type=jnp.float32)
    placed_cols = (
        leaf_map // mid_rows * ncolumns + leaf_parent[:, None]
    ) * mid_rows + leaf_map % mid_rows
    targets = placed_cols.reshape(-1)
    spread = (
        jnp.zeros((nrhs, nmiddle * front), jnp.float32).at[:, targets].add(shares.reshape(nrhs, -1))
    )
    arrived = lax.psum_scatter(spread, ("row", "col"), scatter_dimension=1, tiled=True)
    mid_hb = (mid_grad[:, 0, :].astype(jnp.float32) - arrived).astype(jnp.bfloat16)
    mid_part = jnp.dot(mid_hb, inv_block, preferred_element_type=jnp.float32)
    mid_y = lax.psum_scatter(mid_part, "row", scatter_dimension=1, tiled=True)
    mid_yb = mid_y.astype(jnp.bfloat16)
    mid_share = jnp.dot(mid_yb, cpl_block, preferred_element_type=jnp.float32)
    root_cols = lax.dynamic_index_in_dim(mid_map, col_id, 0, keepdims=False)
    root_term = jnp.zeros((nrhs, root_order), jnp.float32).at[:, root_cols].add(mid_share)
    root_total = lax.psum(root_term, ("row", "col"))
    root_slice = lax.dynamic_slice_in_dim(root_total, row_id * root_rows, root_rows, 1)
    root_hb = (root_grad.astype(jnp.float32) - root_slice).astype(jnp.bfloat16)
    root_y = lax.psum(jnp.dot(root_hb, root_inv, preferred_element_type=jnp.float32), "row")
    root_yb = root_y.astype(jnp.bfloat16)
    root_x = jnp.einsum("kq,pq->kp", root_yb, root_inv, preferred_element_type=jnp.float32)
    root_all = lax.all_gather(root_x.astype(jnp.bfloat16), "row", axis=1, tiled=True)
    coupled = root_all[:, root_cols]
    mid_wb = (
        mid_y - jnp.einsum("kc,bc->kb", coupled, cpl_block, preferred_element_type=jnp.float32)
    ).astype(jnp.bfloat16)
    full_w = lax.all_gather(mid_wb, "row", axis=1, tiled=True)
    mid_x = jnp.einsum("kq,bq->kb", full_w, inv_block, preferred_element_type=jnp.float32)
    all_mid = lax.all_gather(mid_x.astype(jnp.bfloat16), ("row", "col"), axis=1, tiled=True)
    picked = all_mid[:, targets].reshape(nrhs, nleaves, -1)
    leaf_w = leaf_y - jnp.einsum(
        "klc,lpc->lkp", picked, leaf_cpl, preferred_element_type=jnp.float32
    )
    leaf_wb = jnp.where(live, leaf_w, 0.0).astype(jnp.bfloat16)
    leaf_x = jnp.einsum(
        "lkq,lpq->lkp",
        lax.all_gather(leaf_wb, "col", axis=2, tiled=True),
        leaf_inv,
        preferred_element_type=jnp.float32,
    )
    return (leaf_x, mid_x[:, None, :], root_x)


def solution(mesh):
    placed = (
        P("row", None, "col"),
        P("row", "col", None),
        P("row", "col", None),
        P("row"),
        P("row"),
        P("row", None),
        P(None, "col", "row"),
        P("col", "row", None),
        P("col", "row", None),
        P(),
        P(None, "row"),
        P("row", None),
    )
    nrow, ncol = mesh.shape["row"], mesh.shape["col"]

    def run(*args):
        width = args[7].shape[1]
        whole_tiles = width % LANES == 0 and args[0].shape[1] // ncol % 8 == 0
        one_front = args[9].shape[0] == ncol and args[11].shape[0] == width
        if whole_tiles and one_front:
            return fused(nrow, ncol, *args)
        return body(*args)

    return jax.shard_map(
        run,
        mesh=mesh,
        in_specs=placed,
        out_specs=(P("row", None, "col"), P(None, "col", "row"), P(None, "row")),
        check_vma=False,
    )
```

```python
import functools

import jax
import jax.numpy as jnp
from jax import lax
from jax.experimental import pallas as pl
from jax.experimental.pallas import tpu as pltpu
from jax.sharding import PartitionSpec as P

MESH = pl.DeviceIdType.MESH
F32 = jnp.float32
BF16 = jnp.bfloat16
LANES = 128


def dot(a, b):
    return jnp.dot(a, b, preferred_element_type=F32)


def dot_t(a, b):
    return lax.dot_general(a, b, (((1,), (1,)), ((), ())), preferred_element_type=F32)


def pack(x):
    return jnp.concatenate(
        [x[:, i : i + LANES] for i in range(0, x.shape[1], LANES)], axis=0
    )


def kernel(
    nrow,
    ncol,
    grad_hbm,
    inv_hbm,
    cpl_hbm,
    size_hbm,
    parent_hbm,
    map_hbm,
    mgrad_hbm,
    minv_hbm,
    mcpl_hbm,
    mmap_hbm,
    rgrad_hbm,
    rinv_hbm,
    leaf_out,
    mid_out,
    root_out,
    grad_ref,
    map_ref,
    mgrad_ref,
    mmap_ref,
    rgrad_ref,
    inv,
    cpl,
    minv,
    mcpl,
    rinv,
    pick,
    mpick,
    leaf_y,
    rgrad,
    s_fwd,
    r_fwd,
    s_cpl,
    r_cpl,
    s_con,
    r_con,
    s_mid,
    r_mid,
    s_root,
    r_root,
    s_ry,
    r_ry,
    s_rg,
    r_rg,
    s_rx,
    r_rx,
    s_mw,
    r_mw,
    s_mx,
    r_mx,
    s_pk,
    r_pk,
    s_lw,
    r_lw,
    size_ref,
    parent_ref,
    load_sem,
    leaf_sem,
    send_sem,
    recv_sem,
    send_leaf,
    recv_leaf,
):
    ndev = nrow * ncol
    row, col = lax.axis_index("row"), lax.axis_index("col")
    me = row * ncol + col
    nleaf, nrhs, share = grad_ref.shape
    loads = {
        name: pltpu.make_async_copy(src, dst, load_sem.at[i])
        for i, (name, src, dst) in enumerate(
            [
                ("grad", grad_hbm, grad_ref),
                ("map", map_hbm, map_ref),
                ("cpl", cpl_hbm, cpl),
                ("size", size_hbm, size_ref),
                ("parent", parent_hbm, parent_ref),
                ("rgrad", rgrad_hbm, rgrad_ref),
                ("mmap", mmap_hbm, mmap_ref),
                ("mgrad", mgrad_hbm, mgrad_ref),
                ("minv", minv_hbm, minv),
                ("mcpl", mcpl_hbm, mcpl),
                ("rinv", rinv_hbm, rinv),
            ]
        )
    }
    loads["grad"].start()
    inv_loads = [
        pltpu.make_async_copy(inv_hbm.at[f], inv.at[f], leaf_sem.at[f]) for f in range(nleaf)
    ]
    for load in inv_loads:
        load.start()
    for name, load in loads.items():
        if name != "grad":
            load.start()
    kc = nrhs // ncol
    front = minv.shape[1]
    width = minv.shape[0]
    ccols = cpl.shape[2]
    halves = width // LANES

    barrier = pltpu.get_barrier_semaphore()

    def wrap(i, n):
        return jnp.where(i >= n, i - n, i)

    near = [col] + [wrap(col + d, ncol) for d in range(1, ncol)]

    def each(fn):
        def step(t, _):
            orow = wrap(row + t, nrow)
            for d in range(ncol):
                fn(orow, near[d])
            return 0

        lax.fori_loop(1, nrow, step, 0)
        for d in range(1, ncol):
            fn(row, near[d])

    each(
        lambda r, c: pl.semaphore_signal(
            barrier, inc=1, device_id=(r, c), device_id_type=MESH
        )
    )

    def send(phase, src, dst, r, c):
        pltpu.make_async_remote_copy(
            src_ref=src,
            dst_ref=dst,
            send_sem=send_sem.at[phase],
            recv_sem=recv_sem.at[phase],
            device_id=(r, c),
            device_id_type=MESH,
        ).start()

    def to_all(phase, src_of, dst):
        each(lambda r, c: send(phase, src_of(r * ncol + c, c), dst.at[me], r, c))

    def to_rows(phase, src_of, dst):
        def step(t, _):
            orow = wrap(row + t, nrow)
            send(phase, src_of(orow), dst.at[row], orow, col)
            return 0

        lax.fori_loop(1, nrow, step, 0, unroll=True)

    def to_cols(phase, src_of, dst):
        for d in range(1, ncol):
            send(phase, src_of(near[d]), dst.at[col], row, near[d])

    def leaf_copy(turn, f, src, dst, c, slot):
        i = (turn * nleaf + f) * ncol
        return pltpu.make_async_remote_copy(
            src_ref=src,
            dst_ref=dst.at[slot, f],
            send_sem=send_leaf.at[i + c],
            recv_sem=recv_leaf.at[i + slot],
            device_id=(row, c),
            device_id_type=MESH,
        )

    def arrive(phase, dst):
        part = dst.at[pl.ds(0, dst.shape[0] - 1)]
        pltpu.make_async_copy(part, part, recv_sem.at[phase]).wait()

    def sent(phase, dst):
        part = dst.at[pl.ds(0, dst.shape[0] - 1)]
        pltpu.make_async_copy(part, part, send_sem.at[phase]).wait()

    def stage_blocks(buf, t):
        for r in range(nrow):
            for c in range(ncol):
                buf[r * ncol + c] = pack(
                    t[c * kc : (c + 1) * kc, r * width : (r + 1) * width]
                ).astype(BF16)

    def unpack_all(buf):
        x = buf[...].astype(F32)
        x = x.reshape(nrow, ncol, halves, kc, LANES)
        return jnp.concatenate(
            [
                x[r, :, h].reshape(ncol * kc, LANES)
                for r in range(nrow)
                for h in range(halves)
            ],
            axis=1,
        ).astype(BF16)

    loads["grad"].wait()
    for f in range(nleaf):
        inv_loads[f].wait()
        part = dot(grad_ref[f], inv[f])
        for c in range(ncol):
            s_fwd[c, f] = part[:, c * share : (c + 1) * share].astype(BF16)
        if f == 0:
            pl.semaphore_wait(barrier, ndev - 1)
        for c in range(1, ncol):

            @pl.when(col < c)
            def _():
                leaf_copy(0, f, s_fwd.at[c, f], r_fwd, c, col).start()

    loads["map"].wait()

    step_rows = 256

    def fill(i, _):
        rows = pl.ds(pl.multiple_of(i * step_rows, step_rows), step_rows)
        ids = lax.broadcasted_iota(jnp.int32, (step_rows, ccols), 0) + i * step_rows
        for f in range(nleaf):
            pick[rows, f * ccols : (f + 1) * ccols] = jnp.where(
                ids == map_ref[f : f + 1, :], 1.0, 0.0
            ).astype(BF16)
        return 0

    lax.fori_loop(0, front // step_rows, fill, 0)
    loads["rgrad"].wait()
    rgrad[...] = rgrad_ref[...].astype(F32)
    loads["cpl"].wait()
    loads["size"].wait()
    loads["parent"].wait()

    firsts = col * share + lax.broadcasted_iota(jnp.int32, (nrhs, share), 1)
    shares = []
    for f in range(nleaf):
        y = s_fwd[col, f].astype(F32)
        for c in range(ncol - 1):

            @pl.when(col > c)
            def _():
                leaf_copy(0, f, s_fwd.at[c, f], r_fwd, c, c).wait_recv()

            @pl.when(col <= c)
            def _():
                r_fwd[c, f] = jnp.zeros((nrhs, share), BF16)

            y = y + r_fwd[c, f].astype(F32)
        y = jnp.where(firsts < size_ref[f], y, 0.0)
        leaf_y[f] = y
        shares.append(dot(y.astype(BF16), cpl[f]))
    for c in range(ncol):
        s_cpl[c] = jnp.concatenate(
            [u[c * kc : (c + 1) * kc] for u in shares], axis=0
        ).astype(BF16)
    to_cols(0, lambda c: s_cpl.at[c], r_cpl)
    r_cpl[col] = s_cpl[col]

    def fill_mid(i, _):
        rows = pl.ds(pl.multiple_of(i * step_rows, step_rows), step_rows)
        ids = lax.broadcasted_iota(jnp.int32, (step_rows, ccols), 0) + i * step_rows
        mpick[rows, :] = jnp.where(ids == mmap_ref[pl.ds(col, 1), :], 1.0, 0.0).astype(BF16)
        return 0

    loads["mmap"].wait()
    lax.fori_loop(0, front // step_rows, fill_mid, 0)
    for name in ("mgrad", "minv", "mcpl", "rinv"):
        loads[name].wait()

    arrive(0, r_cpl)
    u = r_cpl[0].astype(F32)
    for c in range(1, ncol):
        u = u + r_cpl[c].astype(F32)
    spread = jnp.concatenate(
        [
            jnp.concatenate(
                [
                    jnp.where(parent_ref[f] == p, u[f * kc : (f + 1) * kc], 0.0)
                    for p in range(ncol)
                ],
                axis=0,
            )
            for f in range(nleaf)
        ],
        axis=1,
    ).astype(BF16)
    stage_blocks(s_con, dot_t(spread, pick[...]))
    to_all(1, lambda d, c: s_con.at[d], r_con)
    r_con[me] = s_con[me]

    arrive(1, r_con)
    got = r_con[...].astype(F32).reshape(nrow, ncol, halves, kc, LANES)
    total = got[0]
    for r in range(1, nrow):
        total = total + got[r]
    contrib = jnp.concatenate(
        [total[:, h].reshape(nrhs, LANES) for h in range(halves)], axis=1
    )
    mid_hb = (mgrad_ref[...].astype(F32) - contrib).astype(BF16)
    part = dot(mid_hb, minv[...])
    for r in range(nrow):
        s_mid[r] = part[:, r * width : (r + 1) * width].astype(BF16)
    to_rows(2, lambda r: s_mid.at[r], r_mid)
    r_mid[row] = s_mid[row]
    arrive(2, r_mid)
    mid_y = r_mid[0].astype(F32)
    for r in range(1, nrow):
        mid_y = mid_y + r_mid[r].astype(F32)

    mid_u = dot(mid_y.astype(BF16), mcpl[...])
    stage_blocks(s_root, dot_t(mid_u.astype(BF16), mpick[...]))
    to_all(3, lambda d, c: s_root.at[d], r_root)
    r_root[me] = s_root[me]
    arrive(3, r_root)
    total = jnp.sum(r_root[...].astype(F32), axis=0)
    root_total = jnp.concatenate(
        [total[h * kc : (h + 1) * kc] for h in range(halves)], axis=1
    )
    mine = rgrad[pl.ds(pl.multiple_of(col * kc, kc), kc), :]
    root_hb = (mine - root_total).astype(BF16)
    part = dot(root_hb, rinv[...])
    for r in range(nrow):
        s_ry[r] = pack(part[:, r * width : (r + 1) * width]).astype(BF16)
    to_rows(4, lambda r: s_ry.at[r], r_ry)
    r_ry[row] = s_ry[row]
    arrive(4, r_ry)
    s_rg[...] = jnp.sum(r_ry[...].astype(F32), axis=0).astype(BF16)
    to_rows(5, lambda r: s_rg, r_rg)
    r_rg[row] = s_rg[...]
    arrive(5, r_rg)
    ry = r_rg[...].astype(F32)
    root_yb = jnp.concatenate(
        [ry[r, h * kc : (h + 1) * kc] for r in range(nrow) for h in range(halves)], axis=1
    ).astype(BF16)
    s_rx[...] = pack(dot_t(root_yb, rinv[...])).astype(BF16)
    to_all(6, lambda d, c: s_rx, r_rx)
    r_rx[me] = s_rx[...]
    arrive(6, r_rx)
    root_xb = unpack_all(r_rx)
    own = r_rx[pl.ds(row * ncol, ncol)].astype(F32).reshape(ncol, halves, kc, LANES)
    for h in range(halves):
        root_out[:, h * LANES : (h + 1) * LANES] = own[:, h].reshape(nrhs, LANES)

    coupled = dot(root_xb, mpick[...]).astype(BF16)
    s_mw[...] = (mid_y - dot_t(coupled, mcpl[...])).astype(BF16)
    to_rows(7, lambda r: s_mw, r_mw)
    r_mw[row] = s_mw[...]
    arrive(7, r_mw)
    full_w = jnp.concatenate([r_mw[r] for r in range(nrow)], axis=1)
    mid_x = dot_t(full_w, minv[...])
    mid_out[...] = mid_x
    for c in range(ncol):
        s_mx[c] = pack(mid_x[c * kc : (c + 1) * kc]).astype(BF16)
    to_all(8, lambda d, c: s_mx.at[c], r_mx)
    r_mx[me] = s_mx[col]
    arrive(8, r_mx)

    every = dot(unpack_all(r_mx), pick[...])
    picked = []
    for f in range(nleaf):
        cols = slice(f * ccols, (f + 1) * ccols)
        x = jnp.where(parent_ref[f] == 0, every[0:kc, cols], 0.0)
        for p in range(1, ncol):
            x = jnp.where(parent_ref[f] == p, every[p * kc : (p + 1) * kc, cols], x)
        picked.append(x)
    s_pk[...] = jnp.concatenate(picked, axis=0).astype(BF16)
    to_cols(9, lambda c: s_pk, r_pk)
    r_pk[col] = s_pk[...]
    arrive(9, r_pk)

    got = r_pk[...].astype(F32)
    for f in range(nleaf):
        xb = jnp.concatenate(
            [got[c, f * kc : (f + 1) * kc] for c in range(ncol)], axis=0
        ).astype(BF16)
        w = leaf_y[f] - dot_t(xb, cpl[f])
        s_lw[f] = jnp.where(firsts < size_ref[f], w, 0.0).astype(BF16)
        for c in range(ncol - 1):

            @pl.when(col > c)
            def _():
                leaf_copy(1, f, s_lw.at[f], r_lw, c, col).start()

    for f in range(nleaf):
        r_lw[col, f] = s_lw[f]
        for c in range(ncol):

            @pl.when(col < c)
            def _():
                leaf_copy(1, f, s_lw.at[f], r_lw, c, c).wait_recv()

            @pl.when(col > c)
            def _():
                r_lw[c, f] = jnp.zeros((nrhs, share), BF16)

        w = jnp.concatenate([r_lw[c, f] for c in range(ncol)], axis=1)
        leaf_out[f] = dot_t(w, inv[f])

    for f in range(nleaf):
        for c in range(ncol):

            @pl.when(col < c)
            def _():
                leaf_copy(0, f, s_fwd.at[c, f], r_fwd, c, col).wait_send()

            @pl.when(col > c)
            def _():
                leaf_copy(1, f, s_lw.at[f], r_lw, c, col).wait_send()

    for phase, buf in enumerate(
        [r_cpl, r_con, r_mid, r_root, r_ry, r_rg, r_rx, r_mw, r_mx, r_pk]
    ):
        sent(phase, buf)


def deliver(leaf, mid, root, leaf_out, mid_out, root_out, sem):
    copies = [
        pltpu.make_async_copy(leaf, leaf_out, sem.at[0]),
        pltpu.make_async_copy(root, root_out, sem.at[1]),
    ]
    for copy in copies:
        copy.start()
    mid_out[...] = mid[...][:, None, :]
    for copy in copies:
        copy.wait()


def fused(nrow, ncol, *args):
    (leaf_grad, leaf_inv, leaf_cpl, leaf_size, leaf_parent, leaf_map, mid_grad, mid_inv,
     mid_cpl, mid_map, root_grad, root_inv) = args
    nleaf, nrhs, share = leaf_grad.shape
    order = leaf_inv.shape[2]
    ccols = leaf_cpl.shape[2]
    width, front = mid_inv.shape[1:]
    ndev, kc, halves = nrow * ncol, nrhs // ncol, width // LANES
    vmem = pl.BlockSpec(memory_space=pltpu.VMEM)
    hbm = pl.BlockSpec(memory_space=pltpu.HBM)
    block = (halves * kc, LANES)
    scratch = [
        (leaf_grad.shape, BF16),
        (leaf_map.shape, jnp.int32),
        ((nrhs, width), BF16),
        (mid_map.shape, jnp.int32),
        (root_grad.shape, BF16),
        ((nleaf, share, order), BF16),
        ((nleaf, share, ccols), BF16),
        ((width, front), BF16),
        ((width, mid_cpl.shape[2]), BF16),
        (root_inv.shape, BF16),
        ((front, nleaf * ccols), BF16),
        ((root_inv.shape[1], mid_cpl.shape[2]), BF16),
        ((nleaf, nrhs, share), F32),
        (root_grad.shape, F32),
        ((ncol, nleaf, nrhs, share), BF16),
        ((ncol, nleaf, nrhs, share), BF16),
        ((ncol, nleaf * kc, ccols), BF16),
        ((ncol, nleaf * kc, ccols), BF16),
        ((ndev, *block), BF16),
        ((ndev, *block), BF16),
        ((nrow, nrhs, width), BF16),
        ((nrow, nrhs, width), BF16),
        ((ndev, *block), BF16),
        ((ndev, *block), BF16),
        ((nrow, *block), BF16),
        ((nrow, *block), BF16),
        (block, BF16),
        ((nrow, *block), BF16),
        (block, BF16),
        ((ndev, *block), BF16),
        ((nrhs, width), BF16),
        ((nrow, nrhs, width), BF16),
        ((ncol, *block), BF16),
        ((ndev, *block), BF16),
        ((nleaf * kc, ccols), BF16),
        ((ncol, nleaf * kc, ccols), BF16),
        ((nleaf, nrhs, share), BF16),
        ((ncol, nleaf, nrhs, share), BF16),
    ]
    phases = 10
    leaf_x, mid_x, root_x = pl.pallas_call(
        functools.partial(kernel, nrow, ncol),
        out_shape=(
            jax.ShapeDtypeStruct((nleaf, nrhs, share), F32),
            jax.ShapeDtypeStruct((nrhs, width), F32),
            jax.ShapeDtypeStruct((nrhs, width), F32),
        ),
        in_specs=[hbm] * 12,
        out_specs=(vmem, vmem, vmem),
        scratch_shapes=[pltpu.VMEM(shape, dtype) for shape, dtype in scratch]
        + [
            pltpu.SMEM(leaf_size.shape, jnp.int32),
            pltpu.SMEM(leaf_parent.shape, jnp.int32),
            pltpu.SemaphoreType.DMA((11,)),
            pltpu.SemaphoreType.DMA((nleaf,)),
            pltpu.SemaphoreType.DMA((phases,)),
            pltpu.SemaphoreType.DMA((phases,)),
            pltpu.SemaphoreType.DMA((2 * nleaf * ncol,)),
            pltpu.SemaphoreType.DMA((2 * nleaf * ncol,)),
        ],
        compiler_params=pltpu.CompilerParams(
            collective_id=0, has_side_effects=True, vmem_limit_bytes=63 * 2**20
        ),
    )(
        leaf_grad, leaf_inv, leaf_cpl, leaf_size, leaf_parent, leaf_map, mid_grad[:, 0, :],
        mid_inv[0], mid_cpl[0], mid_map, root_grad, root_inv,
    )
    leaf_x, mid_x, root_x = pl.pallas_call(
        deliver,
        out_shape=(
            jax.ShapeDtypeStruct(leaf_x.shape, F32),
            jax.ShapeDtypeStruct((nrhs, 1, width), F32),
            jax.ShapeDtypeStruct(root_x.shape, F32),
        ),
        in_specs=[pl.BlockSpec(memory_space=pl.ANY), vmem, pl.BlockSpec(memory_space=pl.ANY)],
        out_specs=(hbm, vmem, hbm),
        scratch_shapes=[pltpu.SemaphoreType.DMA((2,))],
        compiler_params=pltpu.CompilerParams(vmem_limit_bytes=63 * 2**20),
    )(leaf_x, mid_x, root_x)
    return leaf_x, mid_x, root_x


def body(
    leaf_grad,
    leaf_inv,
    leaf_cpl,
    leaf_size,
    leaf_parent,
    leaf_map,
    mid_grad,
    mid_inv,
    mid_cpl,
    mid_map,
    root_grad,
    root_inv,
):
    ncolumns = lax.axis_size("col")
    row_id = lax.axis_index("row")
    col_id = lax.axis_index("col")
    nleaves = leaf_inv.shape[0]
    share_rows = leaf_inv.shape[1]
    nrhs = leaf_grad.shape[1]
    front = mid_inv.shape[2]
    mid_rows = mid_inv.shape[1]
    nmiddle = mid_map.shape[0]
    root_order = root_inv.shape[1]
    root_rows = root_inv.shape[0]
    inv_block = mid_inv[0]
    cpl_block = mid_cpl[0]
    first_cols = col_id * share_rows + lax.iota(jnp.int32, share_rows)
    live = (first_cols[None, :] < leaf_size[:, None])[:, None, :]
    partial_value = jnp.einsum(
        "lkp,lpq->lkq", leaf_grad, leaf_inv, preferred_element_type=jnp.float32
    )
    leaf_y = jnp.where(
        live, lax.psum_scatter(partial_value, "col", scatter_dimension=2, tiled=True), 0.0
    )
    leaf_yb = leaf_y.astype(jnp.bfloat16)
    shares = jnp.einsum("lkp,lpc->klc", leaf_yb, leaf_cpl, preferred_element_type=jnp.float32)
    placed_cols = (
        leaf_map // mid_rows * ncolumns + leaf_parent[:, None]
    ) * mid_rows + leaf_map % mid_rows
    targets = placed_cols.reshape(-1)
    spread = (
        jnp.zeros((nrhs, nmiddle * front), jnp.float32).at[:, targets].add(shares.reshape(nrhs, -1))
    )
    arrived = lax.psum_scatter(spread, ("row", "col"), scatter_dimension=1, tiled=True)
    mid_hb = (mid_grad[:, 0, :].astype(jnp.float32) - arrived).astype(jnp.bfloat16)
    mid_part = jnp.dot(mid_hb, inv_block, preferred_element_type=jnp.float32)
    mid_y = lax.psum_scatter(mid_part, "row", scatter_dimension=1, tiled=True)
    mid_yb = mid_y.astype(jnp.bfloat16)
    mid_share = jnp.dot(mid_yb, cpl_block, preferred_element_type=jnp.float32)
    root_cols = lax.dynamic_index_in_dim(mid_map, col_id, 0, keepdims=False)
    root_term = jnp.zeros((nrhs, root_order), jnp.float32).at[:, root_cols].add(mid_share)
    root_total = lax.psum(root_term, ("row", "col"))
    root_slice = lax.dynamic_slice_in_dim(root_total, row_id * root_rows, root_rows, 1)
    root_hb = (root_grad.astype(jnp.float32) - root_slice).astype(jnp.bfloat16)
    root_y = lax.psum(jnp.dot(root_hb, root_inv, preferred_element_type=jnp.float32), "row")
    root_yb = root_y.astype(jnp.bfloat16)
    root_x = jnp.einsum("kq,pq->kp", root_yb, root_inv, preferred_element_type=jnp.float32)
    root_all = lax.all_gather(root_x.astype(jnp.bfloat16), "row", axis=1, tiled=True)
    coupled = root_all[:, root_cols]
    mid_wb = (
        mid_y - jnp.einsum("kc,bc->kb", coupled, cpl_block, preferred_element_type=jnp.float32)
    ).astype(jnp.bfloat16)
    full_w = lax.all_gather(mid_wb, "row", axis=1, tiled=True)
    mid_x = jnp.einsum("kq,bq->kb", full_w, inv_block, preferred_element_type=jnp.float32)
    all_mid = lax.all_gather(mid_x.astype(jnp.bfloat16), ("row", "col"), axis=1, tiled=True)
    picked = all_mid[:, targets].reshape(nrhs, nleaves, -1)
    leaf_w = leaf_y - jnp.einsum(
        "klc,lpc->lkp", picked, leaf_cpl, preferred_element_type=jnp.float32
    )
    leaf_wb = jnp.where(live, leaf_w, 0.0).astype(jnp.bfloat16)
    leaf_x = jnp.einsum(
        "lkq,lpq->lkp",
        lax.all_gather(leaf_wb, "col", axis=2, tiled=True),
        leaf_inv,
        preferred_element_type=jnp.float32,
    )
    return (leaf_x, mid_x[:, None, :], root_x)


def solution(mesh):
    placed = (
        P("row", None, "col"),
        P("row", "col", None),
        P("row", "col", None),
        P("row"),
        P("row"),
        P("row", None),
        P(None, "col", "row"),
        P("col", "row", None),
        P("col", "row", None),
        P(),
        P(None, "row"),
        P("row", None),
    )
    nrow, ncol = mesh.shape["row"], mesh.shape["col"]

    def run(*args):
        width = args[7].shape[1]
        whole_tiles = width % LANES == 0 and args[0].shape[1] // ncol % 8 == 0
        one_front = args[9].shape[0] == ncol and args[11].shape[0] == width
        if whole_tiles and one_front:
            return fused(nrow, ncol, *args)
        return body(*args)

    return jax.shard_map(
        run,
        mesh=mesh,
        in_specs=placed,
        out_specs=(P("row", None, "col"), P(None, "col", "row"), P(None, "row")),
        check_vma=False,
    )
```

```python
import functools

import jax
import jax.numpy as jnp
from jax import lax
from jax.experimental import pallas as pl
from jax.experimental.pallas import tpu as pltpu
from jax.sharding import PartitionSpec as P

MESH = pl.DeviceIdType.MESH
F32 = jnp.float32
BF16 = jnp.bfloat16
LANES = 128


def dot(a, b):
    return jnp.dot(a, b, preferred_element_type=F32)


def dot_t(a, b):
    return lax.dot_general(a, b, (((1,), (1,)), ((), ())), preferred_element_type=F32)


def pack(x):
    return jnp.concatenate(
        [x[:, i : i + LANES] for i in range(0, x.shape[1], LANES)], axis=0
    )


def kernel(
    nrow,
    ncol,
    grad_hbm,
    inv_hbm,
    cpl_hbm,
    size_hbm,
    parent_hbm,
    map_hbm,
    mgrad_hbm,
    minv_hbm,
    mcpl_hbm,
    mmap_hbm,
    rgrad_hbm,
    rinv_hbm,
    leaf_out,
    mid_out,
    root_out,
    grad_ref,
    map_ref,
    mgrad_ref,
    mmap_ref,
    rgrad_ref,
    inv,
    cpl,
    minv,
    mcpl,
    rinv,
    pick,
    mpick,
    leaf_y,
    rgrad,
    s_fwd,
    r_fwd,
    s_cpl,
    r_cpl,
    s_con,
    r_con,
    s_mid,
    r_mid,
    s_root,
    r_root,
    s_ry,
    r_ry,
    s_rx,
    r_rx,
    s_mw,
    r_mw,
    s_mx,
    r_mx,
    s_pk,
    r_pk,
    s_lw,
    r_lw,
    size_ref,
    parent_ref,
    load_sem,
    leaf_sem,
    send_sem,
    recv_sem,
    send_leaf,
    recv_leaf,
    send_row,
    recv_row,
):
    ndev = nrow * ncol
    row, col = lax.axis_index("row"), lax.axis_index("col")
    me = row * ncol + col
    nleaf, nrhs, share = grad_ref.shape
    loads = {
        name: pltpu.make_async_copy(src, dst, load_sem.at[i])
        for i, (name, src, dst) in enumerate(
            [
                ("grad", grad_hbm, grad_ref),
                ("map", map_hbm, map_ref),
                ("cpl", cpl_hbm, cpl),
                ("size", size_hbm, size_ref),
                ("parent", parent_hbm, parent_ref),
                ("rgrad", rgrad_hbm, rgrad_ref),
                ("mmap", mmap_hbm, mmap_ref),
                ("mgrad", mgrad_hbm, mgrad_ref),
                ("minv", minv_hbm, minv),
                ("mcpl", mcpl_hbm, mcpl),
                ("rinv", rinv_hbm, rinv),
            ]
        )
    }
    loads["grad"].start()
    inv_loads = [
        pltpu.make_async_copy(inv_hbm.at[f], inv.at[f], leaf_sem.at[f]) for f in range(nleaf)
    ]
    for load in inv_loads:
        load.start()
    for name, load in loads.items():
        if name != "grad":
            load.start()
    kc = nrhs // ncol
    front = minv.shape[1]
    width = minv.shape[0]
    ccols = cpl.shape[2]
    halves = width // LANES

    r_ry[...] = jnp.zeros(r_ry.shape, BF16)
    barrier = pltpu.get_barrier_semaphore()

    def wrap(i, n):
        return jnp.where(i >= n, i - n, i)

    part_rows = nrow // 2
    own_half = jnp.where(row >= part_rows, part_rows, 0)
    far_half = part_rows - own_half
    place = row - own_half
    near = [col] + [wrap(col + d, ncol) for d in range(1, ncol)]

    def far_rows(fn):
        def step(t, _):
            fn(far_half + wrap(place + t, part_rows))
            return 0

        lax.fori_loop(0, part_rows, step, 0)

    def near_rows(fn):
        def step(t, _):
            fn(own_half + wrap(place + t, part_rows))
            return 0

        lax.fori_loop(1, part_rows, step, 0)

    def each_far(fn):
        far_rows(lambda r: [fn(r, c) for c in near] and None)

    def each_near(fn):
        near_rows(lambda r: [fn(r, c) for c in near] and None)
        for c in near[1:]:
            fn(row, c)

    def each(fn):
        each_far(fn)
        each_near(fn)

    each(
        lambda r, c: pl.semaphore_signal(
            barrier, inc=1, device_id=(r, c), device_id_type=MESH
        )
    )

    def send(phase, src, dst, r, c):
        pltpu.make_async_remote_copy(
            src_ref=src,
            dst_ref=dst,
            send_sem=send_sem.at[phase],
            recv_sem=recv_sem.at[phase],
            device_id=(r, c),
            device_id_type=MESH,
        ).start()

    def to_all(phase, src_of, dst):
        each_far(lambda r, c: send(phase + 1, src_of(c), dst.at[me], r, c))
        each_near(lambda r, c: send(phase, src_of(c), dst.at[me], r, c))

    def to_rows(phase, src, dst):
        far_rows(lambda r: send(phase + 1, src, dst.at[row], r, col))
        near_rows(lambda r: send(phase, src, dst.at[row], r, col))

    def root_copies(r, sender, act):
        first = jnp.maximum(row, r)
        for v in range(nrow):

            @pl.when(first == v)
            def _():
                act(
                    pltpu.make_async_remote_copy(
                        src_ref=s_ry.at[pl.ds(v, nrow - v)],
                        dst_ref=r_ry.at[sender, pl.ds(v, nrow - v)],
                        send_sem=send_row.at[r],
                        recv_sem=recv_row.at[sender],
                        device_id=(r, col),
                        device_id_type=MESH,
                    )
                )

    def to_cols(phase, src_of, dst):
        for d in range(1, ncol):
            send(phase, src_of(near[d]), dst.at[col], row, near[d])

    def leaf_copy(turn, f, src, dst, c, slot):
        i = (turn * nleaf + f) * ncol
        return pltpu.make_async_remote_copy(
            src_ref=src,
            dst_ref=dst.at[slot, f],
            send_sem=send_leaf.at[i + c],
            recv_sem=recv_leaf.at[i + slot],
            device_id=(row, c),
            device_id_type=MESH,
        )

    def some(dst, count):
        part = dst.at[pl.ds(0, count)]
        return part, part

    def arrive(phase, dst, count=None):
        count = dst.shape[0] - 1 if count is None else count
        pltpu.make_async_copy(*some(dst, count), recv_sem.at[phase]).wait()

    def sent(phase, dst, count):
        pltpu.make_async_copy(*some(dst, count), send_sem.at[phase]).wait()

    def halves_of(phase, dst):
        count = dst.shape[0] // 2
        arrive(phase, dst, count - 1)
        yield own_half
        arrive(phase + 1, dst, count)
        yield far_half

    def scatter(phase, x, onehot, buf, dst):
        for half, others in ((far_half, each_far), (own_half, each_near)):
            size = part_rows * width
            places = pl.ds(pl.multiple_of(half * width, size), size)
            t = dot_t(x, onehot[places, :])
            for r in range(part_rows):
                for c in range(ncol):
                    buf[(half + r) * ncol + c] = pack(
                        t[c * kc : (c + 1) * kc, r * width : (r + 1) * width]
                    ).astype(BF16)
            others(lambda r, c: send(phase, buf.at[r * ncol + c], dst.at[me], r, c))
        dst[me] = buf[me]

    def unpack(buf, half):
        x = buf[pl.ds(half * ncol, part_rows * ncol)].astype(F32)
        x = x.reshape(part_rows, ncol, halves, kc, LANES)
        return jnp.concatenate(
            [
                x[r, :, h].reshape(ncol * kc, LANES)
                for r in range(part_rows)
                for h in range(halves)
            ],
            axis=1,
        ).astype(BF16)

    def places_of(half):
        return pl.ds(pl.multiple_of(half * width, part_rows * width), part_rows * width)

    loads["grad"].wait()
    for f in range(nleaf):
        inv_loads[f].wait()
        part = dot(grad_ref[f], inv[f])
        for c in range(ncol):
            s_fwd[c, f] = part[:, c * share : (c + 1) * share].astype(BF16)
        if f == 0:
            pl.semaphore_wait(barrier, ndev - 1)
        for c in range(1, ncol):

            @pl.when(col < c)
            def _():
                leaf_copy(0, f, s_fwd.at[c, f], r_fwd, c, col).start()

    loads["map"].wait()

    step_rows = 256

    def fill(leaves):
        def step(i, _):
            rows = pl.ds(pl.multiple_of(i * step_rows, step_rows), step_rows)
            ids = lax.broadcasted_iota(jnp.int32, (step_rows, ccols), 0) + i * step_rows
            for f in leaves:
                pick[rows, f * ccols : (f + 1) * ccols] = jnp.where(
                    ids == map_ref[f : f + 1, :], 1.0, 0.0
                ).astype(BF16)
            return 0

        lax.fori_loop(0, front // step_rows, step, 0)

    fill(range(nleaf // 2))
    loads["rgrad"].wait()
    rgrad[...] = rgrad_ref[...].astype(F32)
    loads["cpl"].wait()
    loads["size"].wait()
    loads["parent"].wait()

    firsts = col * share + lax.broadcasted_iota(jnp.int32, (nrhs, share), 1)
    shares = []
    for f in range(nleaf):
        y = s_fwd[col, f].astype(F32)
        for c in range(ncol - 1):

            @pl.when(col > c)
            def _():
                leaf_copy(0, f, s_fwd.at[c, f], r_fwd, c, c).wait_recv()

            @pl.when(col <= c)
            def _():
                r_fwd[c, f] = jnp.zeros((nrhs, share), BF16)

            y = y + r_fwd[c, f].astype(F32)
        y = jnp.where(firsts < size_ref[f], y, 0.0)
        leaf_y[f] = y
        shares.append(dot(y.astype(BF16), cpl[f]))
    for c in range(ncol):
        s_cpl[c] = jnp.concatenate(
            [u[c * kc : (c + 1) * kc] for u in shares], axis=0
        ).astype(BF16)
    to_cols(0, lambda c: s_cpl.at[c], r_cpl)
    r_cpl[col] = s_cpl[col]
    fill(range(nleaf // 2, nleaf))

    def fill_mid(i, _):
        rows = pl.ds(pl.multiple_of(i * step_rows, step_rows), step_rows)
        ids = lax.broadcasted_iota(jnp.int32, (step_rows, ccols), 0) + i * step_rows
        mpick[rows, :] = jnp.where(ids == mmap_ref[pl.ds(col, 1), :], 1.0, 0.0).astype(BF16)
        return 0

    arrive(0, r_cpl)
    u = r_cpl[0].astype(F32)
    for c in range(1, ncol):
        u = u + r_cpl[c].astype(F32)
    spread = jnp.concatenate(
        [
            jnp.concatenate(
                [
                    jnp.where(parent_ref[f] == p, u[f * kc : (f + 1) * kc], 0.0)
                    for p in range(ncol)
                ],
                axis=0,
            )
            for f in range(nleaf)
        ],
        axis=1,
    ).astype(BF16)
    scatter(1, spread, pick, s_con, r_con)
    loads["mmap"].wait()
    lax.fori_loop(0, front // step_rows, fill_mid, 0)
    for name in ("mgrad", "minv", "mcpl", "rinv"):
        loads[name].wait()

    arrive(1, r_con)
    got = r_con[...].astype(F32).reshape(nrow, ncol, halves, kc, LANES)
    total = got[0]
    for r in range(1, nrow):
        total = total + got[r]
    contrib = jnp.concatenate(
        [total[:, h].reshape(nrhs, LANES) for h in range(halves)], axis=1
    )
    mid_hb = (mgrad_ref[...].astype(F32) - contrib).astype(BF16)
    for half, others in ((far_half, far_rows), (own_half, near_rows)):
        size = part_rows * width
        part = dot(mid_hb, minv[:, pl.ds(pl.multiple_of(half * width, size), size)])
        for r in range(part_rows):
            s_mid[half + r] = part[:, r * width : (r + 1) * width].astype(BF16)
        others(lambda r: send(2, s_mid.at[r], r_mid.at[row], r, col))
    r_mid[row] = s_mid[row]
    arrive(2, r_mid)
    mid_y = r_mid[0].astype(F32)
    for r in range(1, nrow):
        mid_y = mid_y + r_mid[r].astype(F32)

    mid_u = dot(mid_y.astype(BF16), mcpl[...])
    scatter(3, mid_u.astype(BF16), mpick, s_root, r_root)
    arrive(3, r_root)
    total = jnp.sum(r_root[...].astype(F32), axis=0)
    root_total = jnp.concatenate(
        [total[h * kc : (h + 1) * kc] for h in range(halves)], axis=1
    )
    mine = rgrad[pl.ds(pl.multiple_of(col * kc, kc), kc), :]
    root_hb = (mine - root_total).astype(BF16)
    part = dot(root_hb, rinv[...])
    for r in range(nrow):
        s_ry[r] = pack(part[:, r * width : (r + 1) * width]).astype(BF16)
    far_rows(lambda r: root_copies(r, row, lambda copy: copy.start()))
    near_rows(lambda r: root_copies(r, row, lambda copy: copy.start()))
    r_ry[row] = s_ry[...]
    near_rows(lambda r: root_copies(r, r, lambda copy: copy.wait_recv()))
    far_rows(lambda r: root_copies(r, r, lambda copy: copy.wait_recv()))
    ry = jnp.sum(r_ry[...].astype(F32), axis=0)
    root_yb = jnp.concatenate(
        [ry[r, h * kc : (h + 1) * kc] for r in range(nrow) for h in range(halves)], axis=1
    ).astype(BF16)
    s_rx[...] = pack(dot_t(root_yb, rinv[...])).astype(BF16)
    to_all(4, lambda c: s_rx, r_rx)
    r_rx[me] = s_rx[...]
    coupled = jnp.zeros((nrhs, ccols), F32)
    for half in halves_of(4, r_rx):
        coupled = coupled + dot(unpack(r_rx, half), mpick[places_of(half), :])

    s_mw[...] = (mid_y - dot_t(coupled.astype(BF16), mcpl[...])).astype(BF16)
    to_rows(6, s_mw, r_mw)
    r_mw[row] = s_mw[...]
    own = r_rx[pl.ds(row * ncol, ncol)].astype(F32).reshape(ncol, halves, kc, LANES)
    for h in range(halves):
        root_out[:, h * LANES : (h + 1) * LANES] = own[:, h].reshape(nrhs, LANES)
    mid_x = jnp.zeros((nrhs, width), F32)
    for half in halves_of(6, r_mw):
        w = jnp.concatenate([r_mw[half + r] for r in range(part_rows)], axis=1)
        mid_x = mid_x + dot_t(w, minv[:, places_of(half)])
    for c in range(ncol):
        s_mx[c] = pack(mid_x[c * kc : (c + 1) * kc]).astype(BF16)
    to_all(8, lambda c: s_mx.at[c], r_mx)
    r_mx[me] = s_mx[col]
    mid_out[...] = mid_x

    every = [jnp.zeros((nrhs, ccols), F32)] * nleaf
    for half in halves_of(8, r_mx):
        x = unpack(r_mx, half)
        every = [
            e + dot(x, pick[places_of(half), f * ccols : (f + 1) * ccols])
            for f, e in enumerate(every)
        ]
    batch = nleaf // 2
    for g in range(2):
        picked = []
        for f in range(g * batch, (g + 1) * batch):
            x = jnp.where(parent_ref[f] == 0, every[f][0:kc], 0.0)
            for p in range(1, ncol):
                x = jnp.where(parent_ref[f] == p, every[f][p * kc : (p + 1) * kc], x)
            picked.append(x)
        s_pk[g] = jnp.concatenate(picked, axis=0).astype(BF16)
        to_cols(10 + g, lambda c: s_pk.at[g], r_pk.at[g])
        r_pk[g, col] = s_pk[g]

    for g in range(2):
        arrive(10 + g, r_pk.at[g])
        got = r_pk[g].astype(F32)
        for i in range(batch):
            f = g * batch + i
            xb = jnp.concatenate(
                [got[c, i * kc : (i + 1) * kc] for c in range(ncol)], axis=0
            ).astype(BF16)
            w = leaf_y[f] - dot_t(xb, cpl[f])
            s_lw[f] = jnp.where(firsts < size_ref[f], w, 0.0).astype(BF16)
            for c in range(ncol - 1):

                @pl.when(col > c)
                def _():
                    leaf_copy(1, f, s_lw.at[f], r_lw, c, col).start()

    for f in range(nleaf):
        r_lw[col, f] = s_lw[f]
        for c in range(ncol):

            @pl.when(col < c)
            def _():
                leaf_copy(1, f, s_lw.at[f], r_lw, c, c).wait_recv()

            @pl.when(col > c)
            def _():
                r_lw[c, f] = jnp.zeros((nrhs, share), BF16)

        w = jnp.concatenate([r_lw[c, f] for c in range(ncol)], axis=1)
        leaf_out[f] = dot_t(w, inv[f])

    for f in range(nleaf):
        for c in range(ncol):

            @pl.when(col < c)
            def _():
                leaf_copy(0, f, s_fwd.at[c, f], r_fwd, c, col).wait_send()

            @pl.when(col > c)
            def _():
                leaf_copy(1, f, s_lw.at[f], r_lw, c, col).wait_send()

    for phase, buf in ((0, r_cpl), (1, r_con), (2, r_mid), (3, r_root), (10, r_pk.at[0]), (11, r_pk.at[1])):
        sent(phase, buf, buf.shape[0] - 1)
    for phase, buf in ((4, r_rx), (6, r_mw), (8, r_mx)):
        sent(phase, buf, buf.shape[0] // 2 - 1)
        sent(phase + 1, buf, buf.shape[0] // 2)
    near_rows(lambda r: root_copies(r, row, lambda copy: copy.wait_send()))
    far_rows(lambda r: root_copies(r, row, lambda copy: copy.wait_send()))


def fused(nrow, ncol, *args):
    (leaf_grad, leaf_inv, leaf_cpl, leaf_size, leaf_parent, leaf_map, mid_grad, mid_inv,
     mid_cpl, mid_map, root_grad, root_inv) = args
    nleaf, nrhs, share = leaf_grad.shape
    order = leaf_inv.shape[2]
    ccols = leaf_cpl.shape[2]
    width, front = mid_inv.shape[1:]
    ndev, kc, halves = nrow * ncol, nrhs // ncol, width // LANES
    vmem = pl.BlockSpec(memory_space=pltpu.VMEM)
    hbm = pl.BlockSpec(memory_space=pltpu.HBM)
    block = (halves * kc, LANES)
    scratch = [
        (leaf_grad.shape, BF16),
        (leaf_map.shape, jnp.int32),
        ((nrhs, width), BF16),
        (mid_map.shape, jnp.int32),
        (root_grad.shape, BF16),
        ((nleaf, share, order), BF16),
        ((nleaf, share, ccols), BF16),
        ((width, front), BF16),
        ((width, mid_cpl.shape[2]), BF16),
        (root_inv.shape, BF16),
        ((front, nleaf * ccols), BF16),
        ((root_inv.shape[1], mid_cpl.shape[2]), BF16),
        ((nleaf, nrhs, share), F32),
        (root_grad.shape, F32),
        ((ncol, nleaf, nrhs, share), BF16),
        ((ncol, nleaf, nrhs, share), BF16),
        ((ncol, nleaf * kc, ccols), BF16),
        ((ncol, nleaf * kc, ccols), BF16),
        ((ndev, *block), BF16),
        ((ndev, *block), BF16),
        ((nrow, nrhs, width), BF16),
        ((nrow, nrhs, width), BF16),
        ((ndev, *block), BF16),
        ((ndev, *block), BF16),
        ((nrow, *block), BF16),
        ((nrow, nrow, *block), BF16),
        (block, BF16),
        ((ndev, *block), BF16),
        ((nrhs, width), BF16),
        ((nrow, nrhs, width), BF16),
        ((ncol, *block), BF16),
        ((ndev, *block), BF16),
        ((2, nleaf * kc // 2, ccols), BF16),
        ((2, ncol, nleaf * kc // 2, ccols), BF16),
        ((nleaf, nrhs, share), BF16),
        ((ncol, nleaf, nrhs, share), BF16),
    ]
    phases = 12
    leaf_x, mid_x, root_x = pl.pallas_call(
        functools.partial(kernel, nrow, ncol),
        out_shape=(
            jax.ShapeDtypeStruct((nleaf, nrhs, share), F32),
            jax.ShapeDtypeStruct((nrhs, width), F32),
            jax.ShapeDtypeStruct((nrhs, width), F32),
        ),
        in_specs=[hbm] * 12,
        out_specs=(vmem, vmem, vmem),
        scratch_shapes=[pltpu.VMEM(shape, dtype) for shape, dtype in scratch]
        + [
            pltpu.SMEM(leaf_size.shape, jnp.int32),
            pltpu.SMEM(leaf_parent.shape, jnp.int32),
            pltpu.SemaphoreType.DMA((11,)),
            pltpu.SemaphoreType.DMA((nleaf,)),
            pltpu.SemaphoreType.DMA((phases,)),
            pltpu.SemaphoreType.DMA((phases,)),
            pltpu.SemaphoreType.DMA((2 * nleaf * ncol,)),
            pltpu.SemaphoreType.DMA((2 * nleaf * ncol,)),
            pltpu.SemaphoreType.DMA((nrow,)),
            pltpu.SemaphoreType.DMA((nrow,)),
        ],
        compiler_params=pltpu.CompilerParams(
            collective_id=0, has_side_effects=True, vmem_limit_bytes=63 * 2**20
        ),
    )(
        leaf_grad, leaf_inv, leaf_cpl, leaf_size, leaf_parent, leaf_map, mid_grad[:, 0, :],
        mid_inv[0], mid_cpl[0], mid_map, root_grad, root_inv,
    )
    return leaf_x, mid_x[:, None, :], root_x


def body(
    leaf_grad,
    leaf_inv,
    leaf_cpl,
    leaf_size,
    leaf_parent,
    leaf_map,
    mid_grad,
    mid_inv,
    mid_cpl,
    mid_map,
    root_grad,
    root_inv,
):
    ncolumns = lax.axis_size("col")
    row_id = lax.axis_index("row")
    col_id = lax.axis_index("col")
    nleaves = leaf_inv.shape[0]
    share_rows = leaf_inv.shape[1]
    nrhs = leaf_grad.shape[1]
    front = mid_inv.shape[2]
    mid_rows = mid_inv.shape[1]
    nmiddle = mid_map.shape[0]
    root_order = root_inv.shape[1]
    root_rows = root_inv.shape[0]
    inv_block = mid_inv[0]
    cpl_block = mid_cpl[0]
    first_cols = col_id * share_rows + lax.iota(jnp.int32, share_rows)
    live = (first_cols[None, :] < leaf_size[:, None])[:, None, :]
    partial_value = jnp.einsum(
        "lkp,lpq->lkq", leaf_grad, leaf_inv, preferred_element_type=jnp.float32
    )
    leaf_y = jnp.where(
        live, lax.psum_scatter(partial_value, "col", scatter_dimension=2, tiled=True), 0.0
    )
    leaf_yb = leaf_y.astype(jnp.bfloat16)
    shares = jnp.einsum("lkp,lpc->klc", leaf_yb, leaf_cpl, preferred_element_type=jnp.float32)
    placed_cols = (
        leaf_map // mid_rows * ncolumns + leaf_parent[:, None]
    ) * mid_rows + leaf_map % mid_rows
    targets = placed_cols.reshape(-1)
    spread = (
        jnp.zeros((nrhs, nmiddle * front), jnp.float32).at[:, targets].add(shares.reshape(nrhs, -1))
    )
    arrived = lax.psum_scatter(spread, ("row", "col"), scatter_dimension=1, tiled=True)
    mid_hb = (mid_grad[:, 0, :].astype(jnp.float32) - arrived).astype(jnp.bfloat16)
    mid_part = jnp.dot(mid_hb, inv_block, preferred_element_type=jnp.float32)
    mid_y = lax.psum_scatter(mid_part, "row", scatter_dimension=1, tiled=True)
    mid_yb = mid_y.astype(jnp.bfloat16)
    mid_share = jnp.dot(mid_yb, cpl_block, preferred_element_type=jnp.float32)
    root_cols = lax.dynamic_index_in_dim(mid_map, col_id, 0, keepdims=False)
    root_term = jnp.zeros((nrhs, root_order), jnp.float32).at[:, root_cols].add(mid_share)
    root_total = lax.psum(root_term, ("row", "col"))
    root_slice = lax.dynamic_slice_in_dim(root_total, row_id * root_rows, root_rows, 1)
    root_hb = (root_grad.astype(jnp.float32) - root_slice).astype(jnp.bfloat16)
    root_y = lax.psum(jnp.dot(root_hb, root_inv, preferred_element_type=jnp.float32), "row")
    root_yb = root_y.astype(jnp.bfloat16)
    root_x = jnp.einsum("kq,pq->kp", root_yb, root_inv, preferred_element_type=jnp.float32)
    root_all = lax.all_gather(root_x.astype(jnp.bfloat16), "row", axis=1, tiled=True)
    coupled = root_all[:, root_cols]
    mid_wb = (
        mid_y - jnp.einsum("kc,bc->kb", coupled, cpl_block, preferred_element_type=jnp.float32)
    ).astype(jnp.bfloat16)
    full_w = lax.all_gather(mid_wb, "row", axis=1, tiled=True)
    mid_x = jnp.einsum("kq,bq->kb", full_w, inv_block, preferred_element_type=jnp.float32)
    all_mid = lax.all_gather(mid_x.astype(jnp.bfloat16), ("row", "col"), axis=1, tiled=True)
    picked = all_mid[:, targets].reshape(nrhs, nleaves, -1)
    leaf_w = leaf_y - jnp.einsum(
        "klc,lpc->lkp", picked, leaf_cpl, preferred_element_type=jnp.float32
    )
    leaf_wb = jnp.where(live, leaf_w, 0.0).astype(jnp.bfloat16)
    leaf_x = jnp.einsum(
        "lkq,lpq->lkp",
        lax.all_gather(leaf_wb, "col", axis=2, tiled=True),
        leaf_inv,
        preferred_element_type=jnp.float32,
    )
    return (leaf_x, mid_x[:, None, :], root_x)


def solution(mesh):
    placed = (
        P("row", None, "col"),
        P("row", "col", None),
        P("row", "col", None),
        P("row"),
        P("row"),
        P("row", None),
        P(None, "col", "row"),
        P("col", "row", None),
        P("col", "row", None),
        P(),
        P(None, "row"),
        P("row", None),
    )
    nrow, ncol = mesh.shape["row"], mesh.shape["col"]

    def run(*args):
        width = args[7].shape[1]
        kc, nleaf = args[0].shape[1] // ncol, args[0].shape[0]
        whole_tiles = width % LANES == 0 and kc % 8 == 0 and nleaf * kc % 32 == 0 and width * kc % 2048 == 0
        one_front = args[9].shape[0] == ncol and args[11].shape[0] == width
        if whole_tiles and one_front and nrow % 2 == 0 and nleaf % 2 == 0:
            return fused(nrow, ncol, *args)
        return body(*args)

    return jax.shard_map(
        run,
        mesh=mesh,
        in_specs=placed,
        out_specs=(P("row", None, "col"), P(None, "col", "row"), P(None, "row")),
        check_vma=False,
    )
```

```python
import functools

import jax
import jax.numpy as jnp
from jax import lax
from jax.experimental import pallas as pl
from jax.experimental.pallas import tpu as pltpu
from jax.sharding import PartitionSpec as P

MESH = pl.DeviceIdType.MESH
F32 = jnp.float32
BF16 = jnp.bfloat16
LANES = 128


def dot(a, b):
    return jnp.dot(a, b, preferred_element_type=F32)


def pack(x):
    return jnp.concatenate(
        [x[:, i : i + LANES] for i in range(0, x.shape[1], LANES)], axis=0
    )


def kernel(
    nrow,
    ncol,
    grad_hbm,
    inv_hbm,
    cpl_hbm,
    size_hbm,
    parent_hbm,
    map_hbm,
    mgrad_hbm,
    minv_hbm,
    mcpl_hbm,
    mmap_hbm,
    rgrad_hbm,
    rinv_hbm,
    leaf_out,
    mid_out,
    root_out,
    grad_ref,
    map_ref,
    mgrad_ref,
    mmap_ref,
    rgrad_ref,
    inv,
    cpl,
    minv,
    mcpl,
    rinv,
    cpl_t,
    inv_t,
    minv_t,
    mcpl_t,
    rinv_t,
    place_one,
    mplace,
    pick,
    mpick,
    leaf_y,
    rgrad,
    s_fwd,
    r_fwd,
    s_cpl,
    r_cpl,
    s_con,
    r_con,
    s_mid,
    r_mid,
    s_root,
    r_root,
    s_ry,
    r_ry,
    s_rx,
    r_rx,
    s_mw,
    r_mw,
    s_mx,
    r_mx,
    s_pk,
    r_pk,
    s_lw,
    r_lw,
    size_ref,
    parent_ref,
    load_sem,
    leaf_sem,
    send_sem,
    recv_sem,
    send_leaf,
    recv_leaf,
    send_row,
    recv_row,
):
    ndev = nrow * ncol
    row, col = lax.axis_index("row"), lax.axis_index("col")
    me = row * ncol + col
    nleaf, nrhs, share = grad_ref.shape
    loads = {
        name: pltpu.make_async_copy(src, dst, load_sem.at[i])
        for i, (name, src, dst) in enumerate(
            [
                ("grad", grad_hbm, grad_ref),
                ("map", map_hbm, map_ref),
                ("cpl", cpl_hbm, cpl),
                ("size", size_hbm, size_ref),
                ("parent", parent_hbm, parent_ref),
                ("rgrad", rgrad_hbm, rgrad_ref),
                ("mmap", mmap_hbm, mmap_ref),
                ("mgrad", mgrad_hbm, mgrad_ref),
                ("minv", minv_hbm, minv),
                ("mcpl", mcpl_hbm, mcpl),
                ("rinv", rinv_hbm, rinv),
            ]
        )
    }
    loads["grad"].start()
    inv_loads = [
        pltpu.make_async_copy(inv_hbm.at[f], inv.at[f], leaf_sem.at[f]) for f in range(nleaf)
    ]
    for load in inv_loads:
        load.start()
    for name, load in loads.items():
        if name != "grad":
            load.start()
    kc = nrhs // ncol
    front = minv.shape[1]
    width = minv.shape[0]
    ccols = cpl.shape[2]
    halves = width // LANES

    r_ry[...] = jnp.zeros(r_ry.shape, BF16)
    barrier = pltpu.get_barrier_semaphore()

    def wrap(i, n):
        return jnp.where(i >= n, i - n, i)

    part_rows = nrow // 2
    own_half = jnp.where(row >= part_rows, part_rows, 0)
    far_half = part_rows - own_half
    place = row - own_half
    near = [col] + [wrap(col + d, ncol) for d in range(1, ncol)]

    def far_rows(fn):
        def step(t, _):
            fn(far_half + wrap(place + t, part_rows))
            return 0

        lax.fori_loop(0, part_rows, step, 0)

    def near_rows(fn):
        def step(t, _):
            fn(own_half + wrap(place + t, part_rows))
            return 0

        lax.fori_loop(1, part_rows, step, 0)

    def each_far(fn):
        far_rows(lambda r: [fn(r, c) for c in near] and None)

    def each_near(fn):
        near_rows(lambda r: [fn(r, c) for c in near] and None)
        for c in near[1:]:
            fn(row, c)

    def each(fn):
        each_far(fn)
        each_near(fn)

    each(
        lambda r, c: pl.semaphore_signal(
            barrier, inc=1, device_id=(r, c), device_id_type=MESH
        )
    )

    def send(phase, src, dst, r, c):
        pltpu.make_async_remote_copy(
            src_ref=src,
            dst_ref=dst,
            send_sem=send_sem.at[phase],
            recv_sem=recv_sem.at[phase],
            device_id=(r, c),
            device_id_type=MESH,
        ).start()

    def to_all(phase, src_of, dst):
        each_far(lambda r, c: send(phase + 1, src_of(c), dst.at[me], r, c))
        each_near(lambda r, c: send(phase, src_of(c), dst.at[me], r, c))

    def to_rows(phase, src, dst):
        far_rows(lambda r: send(phase + 1, src, dst.at[row], r, col))
        near_rows(lambda r: send(phase, src, dst.at[row], r, col))

    def root_copies(r, sender, act):
        first = jnp.maximum(row, r)
        for v in range(nrow):

            @pl.when(first == v)
            def _():
                act(
                    pltpu.make_async_remote_copy(
                        src_ref=s_ry.at[pl.ds(v, nrow - v)],
                        dst_ref=r_ry.at[sender, pl.ds(v, nrow - v)],
                        send_sem=send_row.at[r],
                        recv_sem=recv_row.at[sender],
                        device_id=(r, col),
                        device_id_type=MESH,
                    )
                )

    def to_cols(phase, src_of, dst):
        for d in range(1, ncol):
            send(phase, src_of(near[d]), dst.at[col], row, near[d])

    def leaf_copy(turn, f, src, dst, c, slot):
        i = (turn * nleaf + f) * ncol
        return pltpu.make_async_remote_copy(
            src_ref=src,
            dst_ref=dst.at[slot, f],
            send_sem=send_leaf.at[i + c],
            recv_sem=recv_leaf.at[i + slot],
            device_id=(row, c),
            device_id_type=MESH,
        )

    def some(dst, count):
        part = dst.at[pl.ds(0, count)]
        return part, part

    def arrive(phase, dst, count=None):
        count = dst.shape[0] - 1 if count is None else count
        pltpu.make_async_copy(*some(dst, count), recv_sem.at[phase]).wait()

    def sent(phase, dst, count):
        pltpu.make_async_copy(*some(dst, count), send_sem.at[phase]).wait()

    def halves_of(phase, dst):
        count = dst.shape[0] // 2
        arrive(phase, dst, count - 1)
        yield own_half
        arrive(phase + 1, dst, count)
        yield far_half

    def scatter(phase, x, onehot, buf, dst):
        for half, others in ((far_half, each_far), (own_half, each_near)):
            size = part_rows * width
            places = pl.ds(pl.multiple_of(half * width, size), size)
            t = dot(x, onehot[:, places])
            for r in range(part_rows):
                for c in range(ncol):
                    buf[(half + r) * ncol + c] = pack(
                        t[c * kc : (c + 1) * kc, r * width : (r + 1) * width]
                    ).astype(BF16)
            others(lambda r, c: send(phase, buf.at[r * ncol + c], dst.at[me], r, c))
        dst[me] = buf[me]

    def unpack(buf, half):
        x = buf[pl.ds(half * ncol, part_rows * ncol)].astype(F32)
        x = x.reshape(part_rows, ncol, halves, kc, LANES)
        return jnp.concatenate(
            [
                x[r, :, h].reshape(ncol * kc, LANES)
                for r in range(part_rows)
                for h in range(halves)
            ],
            axis=1,
        ).astype(BF16)

    def places_of(half):
        return pl.ds(pl.multiple_of(half * width, part_rows * width), part_rows * width)

    loads["grad"].wait()
    for f in range(nleaf):
        inv_loads[f].wait()
        part = dot(grad_ref[f], inv[f])
        for c in range(ncol):
            s_fwd[c, f] = part[:, c * share : (c + 1) * share].astype(BF16)
        if f == 0:
            pl.semaphore_wait(barrier, ndev - 1)
        for c in range(1, ncol):

            @pl.when(col < c)
            def _():
                leaf_copy(0, f, s_fwd.at[c, f], r_fwd, c, col).start()

    loads["map"].wait()

    step_rows = 256

    def fill(row_map, dst, first):
        def step(i, _):
            rows = pl.ds(pl.multiple_of(i * step_rows, step_rows), step_rows)
            ids = lax.broadcasted_iota(jnp.int32, (step_rows, ccols), 0) + i * step_rows
            dst[rows, first : first + ccols] = jnp.where(ids == row_map, 1.0, 0.0).astype(BF16)
            return 0

        lax.fori_loop(0, front // step_rows, step, 0)

    def fill_t(row_map, dst, first):
        down = jnp.broadcast_to(row_map.astype(F32), (LANES, ccols)).T.astype(jnp.int32)
        ids = lax.broadcasted_iota(jnp.int32, (ccols, LANES), 1)

        def step(i, _):
            across = pl.ds(pl.multiple_of(i * LANES, LANES), LANES)
            dst[first : first + ccols, across] = jnp.where(
                ids + i * LANES == down, 1.0, 0.0
            ).astype(BF16)
            return 0

        lax.fori_loop(0, front // LANES, step, 0)

    def leaf_map_of(f):
        return map_ref[f : f + 1, :]

    for f in range(nleaf // 2):
        fill_t(leaf_map_of(f), place_one, f * ccols)
    loads["rgrad"].wait()
    rgrad[...] = rgrad_ref[...].astype(F32)
    loads["cpl"].wait()
    loads["size"].wait()
    loads["parent"].wait()

    firsts = col * share + lax.broadcasted_iota(jnp.int32, (nrhs, share), 1)
    shares = []
    for f in range(nleaf):
        y = s_fwd[col, f].astype(F32)
        for c in range(ncol - 1):

            @pl.when(col > c)
            def _():
                leaf_copy(0, f, s_fwd.at[c, f], r_fwd, c, c).wait_recv()

            @pl.when(col <= c)
            def _():
                r_fwd[c, f] = jnp.zeros((nrhs, share), BF16)

            y = y + r_fwd[c, f].astype(F32)
        y = jnp.where(firsts < size_ref[f], y, 0.0)
        leaf_y[f] = y
        shares.append(dot(y.astype(BF16), cpl[f]))
    for c in range(ncol):
        s_cpl[c] = jnp.concatenate(
            [u[c * kc : (c + 1) * kc] for u in shares], axis=0
        ).astype(BF16)
    to_cols(0, lambda c: s_cpl.at[c], r_cpl)
    r_cpl[col] = s_cpl[col]
    for f in range(nleaf // 2, nleaf):
        fill_t(leaf_map_of(f), place_one, f * ccols)

    arrive(0, r_cpl)
    u = r_cpl[0].astype(F32)
    for c in range(1, ncol):
        u = u + r_cpl[c].astype(F32)
    spread = jnp.concatenate(
        [
            jnp.concatenate(
                [
                    jnp.where(parent_ref[f] == p, u[f * kc : (f + 1) * kc], 0.0)
                    for p in range(ncol)
                ],
                axis=0,
            )
            for f in range(nleaf)
        ],
        axis=1,
    ).astype(BF16)
    scatter(1, spread, place_one, s_con, r_con)
    loads["mmap"].wait()
    fill_t(mmap_ref[pl.ds(col, 1), :], mplace, 0)
    for name in ("mgrad", "minv", "mcpl", "rinv"):
        loads[name].wait()

    arrive(1, r_con)
    got = r_con[...].astype(F32).reshape(nrow, ncol, halves, kc, LANES)
    total = got[0]
    for r in range(1, nrow):
        total = total + got[r]
    contrib = jnp.concatenate(
        [total[:, h].reshape(nrhs, LANES) for h in range(halves)], axis=1
    )
    mid_hb = (mgrad_ref[...].astype(F32) - contrib).astype(BF16)
    for half, others in ((far_half, far_rows), (own_half, near_rows)):
        size = part_rows * width
        part = dot(mid_hb, minv[:, pl.ds(pl.multiple_of(half * width, size), size)])
        for r in range(part_rows):
            s_mid[half + r] = part[:, r * width : (r + 1) * width].astype(BF16)
        others(lambda r: send(2, s_mid.at[r], r_mid.at[row], r, col))
    r_mid[row] = s_mid[row]
    fill(mmap_ref[pl.ds(col, 1), :], mpick, 0)
    for f in range(nleaf // 2):
        fill(leaf_map_of(f), pick, f * ccols)
    arrive(2, r_mid)
    mid_y = r_mid[0].astype(F32)
    for r in range(1, nrow):
        mid_y = mid_y + r_mid[r].astype(F32)

    mid_u = dot(mid_y.astype(BF16), mcpl[...])
    scatter(3, mid_u.astype(BF16), mplace, s_root, r_root)
    rinv_t[...] = rinv[...].T
    for f in range(nleaf // 2, nleaf):
        fill(leaf_map_of(f), pick, f * ccols)
    arrive(3, r_root)
    total = jnp.sum(r_root[...].astype(F32), axis=0)
    root_total = jnp.concatenate(
        [total[h * kc : (h + 1) * kc] for h in range(halves)], axis=1
    )
    mine = rgrad[pl.ds(pl.multiple_of(col * kc, kc), kc), :]
    root_hb = (mine - root_total).astype(BF16)
    part = dot(root_hb, rinv[...])
    for r in range(nrow):
        s_ry[r] = pack(part[:, r * width : (r + 1) * width]).astype(BF16)
    far_rows(lambda r: root_copies(r, row, lambda copy: copy.start()))
    near_rows(lambda r: root_copies(r, row, lambda copy: copy.start()))
    r_ry[row] = s_ry[...]
    minv_t[...] = minv[...].T
    mcpl_t[...] = mcpl[...].T
    near_rows(lambda r: root_copies(r, r, lambda copy: copy.wait_recv()))
    far_rows(lambda r: root_copies(r, r, lambda copy: copy.wait_recv()))
    ry = jnp.sum(r_ry[...].astype(F32), axis=0)
    root_yb = jnp.concatenate(
        [ry[r, h * kc : (h + 1) * kc] for r in range(nrow) for h in range(halves)], axis=1
    ).astype(BF16)
    s_rx[...] = pack(dot(root_yb, rinv_t[...])).astype(BF16)
    to_all(4, lambda c: s_rx, r_rx)
    r_rx[me] = s_rx[...]
    for f in range(nleaf):
        cpl_t[f] = cpl[f].T
    coupled = jnp.zeros((nrhs, ccols), F32)
    for half in halves_of(4, r_rx):
        coupled = coupled + dot(unpack(r_rx, half), mpick[places_of(half), :])

    s_mw[...] = (mid_y - dot(coupled.astype(BF16), mcpl_t[...])).astype(BF16)
    to_rows(6, s_mw, r_mw)
    r_mw[row] = s_mw[...]
    own = r_rx[pl.ds(row * ncol, ncol)].astype(F32).reshape(ncol, halves, kc, LANES)
    for h in range(halves):
        root_out[:, h * LANES : (h + 1) * LANES] = own[:, h].reshape(nrhs, LANES)
    for f in range(nleaf):
        inv_t[f] = inv[f].T
    mid_x = jnp.zeros((nrhs, width), F32)
    for half in halves_of(6, r_mw):
        w = jnp.concatenate([r_mw[half + r] for r in range(part_rows)], axis=1)
        mid_x = mid_x + dot(w, minv_t[places_of(half), :])
    for c in range(ncol):
        s_mx[c] = pack(mid_x[c * kc : (c + 1) * kc]).astype(BF16)
    to_all(8, lambda c: s_mx.at[c], r_mx)
    r_mx[me] = s_mx[col]
    mid_out[...] = mid_x

    every = [jnp.zeros((nrhs, ccols), F32)] * nleaf
    for half in halves_of(8, r_mx):
        x = unpack(r_mx, half)
        every = [
            e + dot(x, pick[places_of(half), f * ccols : (f + 1) * ccols])
            for f, e in enumerate(every)
        ]
    batch = nleaf // 2
    for g in range(2):
        picked = []
        for f in range(g * batch, (g + 1) * batch):
            x = jnp.where(parent_ref[f] == 0, every[f][0:kc], 0.0)
            for p in range(1, ncol):
                x = jnp.where(parent_ref[f] == p, every[f][p * kc : (p + 1) * kc], x)
            picked.append(x)
        s_pk[g] = jnp.concatenate(picked, axis=0).astype(BF16)
        to_cols(10 + g, lambda c: s_pk.at[g], r_pk.at[g])
        r_pk[g, col] = s_pk[g]

    for g in range(2):
        arrive(10 + g, r_pk.at[g])
        got = r_pk[g].astype(F32)
        for i in range(batch):
            f = g * batch + i
            xb = jnp.concatenate(
                [got[c, i * kc : (i + 1) * kc] for c in range(ncol)], axis=0
            ).astype(BF16)
            w = leaf_y[f] - dot(xb, cpl_t[f])
            s_lw[f] = jnp.where(firsts < size_ref[f], w, 0.0).astype(BF16)
            for c in range(ncol - 1):

                @pl.when(col > c)
                def _():
                    leaf_copy(1, f, s_lw.at[f], r_lw, c, col).start()

    for f in range(nleaf):
        r_lw[col, f] = s_lw[f]
        for c in range(ncol):

            @pl.when(col < c)
            def _():
                leaf_copy(1, f, s_lw.at[f], r_lw, c, c).wait_recv()

            @pl.when(col > c)
            def _():
                r_lw[c, f] = jnp.zeros((nrhs, share), BF16)

        w = jnp.concatenate([r_lw[c, f] for c in range(ncol)], axis=1)
        leaf_out[f] = dot(w, inv_t[f])

    for f in range(nleaf):
        for c in range(ncol):

            @pl.when(col < c)
            def _():
                leaf_copy(0, f, s_fwd.at[c, f], r_fwd, c, col).wait_send()

            @pl.when(col > c)
            def _():
                leaf_copy(1, f, s_lw.at[f], r_lw, c, col).wait_send()

    for phase, buf in ((0, r_cpl), (1, r_con), (2, r_mid), (3, r_root), (10, r_pk.at[0]), (11, r_pk.at[1])):
        sent(phase, buf, buf.shape[0] - 1)
    for phase, buf in ((4, r_rx), (6, r_mw), (8, r_mx)):
        sent(phase, buf, buf.shape[0] // 2 - 1)
        sent(phase + 1, buf, buf.shape[0] // 2)
    near_rows(lambda r: root_copies(r, row, lambda copy: copy.wait_send()))
    far_rows(lambda r: root_copies(r, row, lambda copy: copy.wait_send()))


def fused(nrow, ncol, *args):
    (leaf_grad, leaf_inv, leaf_cpl, leaf_size, leaf_parent, leaf_map, mid_grad, mid_inv,
     mid_cpl, mid_map, root_grad, root_inv) = args
    nleaf, nrhs, share = leaf_grad.shape
    order = leaf_inv.shape[2]
    ccols = leaf_cpl.shape[2]
    width, front = mid_inv.shape[1:]
    ndev, kc, halves = nrow * ncol, nrhs // ncol, width // LANES
    vmem = pl.BlockSpec(memory_space=pltpu.VMEM)
    hbm = pl.BlockSpec(memory_space=pltpu.HBM)
    block = (halves * kc, LANES)
    scratch = [
        (leaf_grad.shape, BF16),
        (leaf_map.shape, jnp.int32),
        ((nrhs, width), BF16),
        (mid_map.shape, jnp.int32),
        (root_grad.shape, BF16),
        ((nleaf, share, order), BF16),
        ((nleaf, share, ccols), BF16),
        ((width, front), BF16),
        ((width, mid_cpl.shape[2]), BF16),
        (root_inv.shape, BF16),
        ((nleaf, ccols, share), BF16),
        ((nleaf, order, share), BF16),
        ((front, width), BF16),
        ((mid_cpl.shape[2], width), BF16),
        (root_inv.shape[::-1], BF16),
        ((nleaf * ccols, front), BF16),
        ((mid_cpl.shape[2], root_inv.shape[1]), BF16),
        ((front, nleaf * ccols), BF16),
        ((root_inv.shape[1], mid_cpl.shape[2]), BF16),
        ((nleaf, nrhs, share), F32),
        (root_grad.shape, F32),
        ((ncol, nleaf, nrhs, share), BF16),
        ((ncol, nleaf, nrhs, share), BF16),
        ((ncol, nleaf * kc, ccols), BF16),
        ((ncol, nleaf * kc, ccols), BF16),
        ((ndev, *block), BF16),
        ((ndev, *block), BF16),
        ((nrow, nrhs, width), BF16),
        ((nrow, nrhs, width), BF16),
        ((ndev, *block), BF16),
        ((ndev, *block), BF16),
        ((nrow, *block), BF16),
        ((nrow, nrow, *block), BF16),
        (block, BF16),
        ((ndev, *block), BF16),
        ((nrhs, width), BF16),
        ((nrow, nrhs, width), BF16),
        ((ncol, *block), BF16),
        ((ndev, *block), BF16),
        ((2, nleaf * kc // 2, ccols), BF16),
        ((2, ncol, nleaf * kc // 2, ccols), BF16),
        ((nleaf, nrhs, share), BF16),
        ((ncol, nleaf, nrhs, share), BF16),
    ]
    phases = 12
    leaf_x, mid_x, root_x = pl.pallas_call(
        functools.partial(kernel, nrow, ncol),
        out_shape=(
            jax.ShapeDtypeStruct((nleaf, nrhs, share), F32),
            jax.ShapeDtypeStruct((nrhs, width), F32),
            jax.ShapeDtypeStruct((nrhs, width), F32),
        ),
        in_specs=[hbm] * 12,
        out_specs=(vmem, vmem, vmem),
        scratch_shapes=[pltpu.VMEM(shape, dtype) for shape, dtype in scratch]
        + [
            pltpu.SMEM(leaf_size.shape, jnp.int32),
            pltpu.SMEM(leaf_parent.shape, jnp.int32),
            pltpu.SemaphoreType.DMA((11,)),
            pltpu.SemaphoreType.DMA((nleaf,)),
            pltpu.SemaphoreType.DMA((phases,)),
            pltpu.SemaphoreType.DMA((phases,)),
            pltpu.SemaphoreType.DMA((2 * nleaf * ncol,)),
            pltpu.SemaphoreType.DMA((2 * nleaf * ncol,)),
            pltpu.SemaphoreType.DMA((nrow,)),
            pltpu.SemaphoreType.DMA((nrow,)),
        ],
        compiler_params=pltpu.CompilerParams(
            collective_id=0, has_side_effects=True, vmem_limit_bytes=63 * 2**20
        ),
    )(
        leaf_grad, leaf_inv, leaf_cpl, leaf_size, leaf_parent, leaf_map, mid_grad[:, 0, :],
        mid_inv[0], mid_cpl[0], mid_map, root_grad, root_inv,
    )
    return leaf_x, mid_x[:, None, :], root_x


def body(
    leaf_grad,
    leaf_inv,
    leaf_cpl,
    leaf_size,
    leaf_parent,
    leaf_map,
    mid_grad,
    mid_inv,
    mid_cpl,
    mid_map,
    root_grad,
    root_inv,
):
    ncolumns = lax.axis_size("col")
    row_id = lax.axis_index("row")
    col_id = lax.axis_index("col")
    nleaves = leaf_inv.shape[0]
    share_rows = leaf_inv.shape[1]
    nrhs = leaf_grad.shape[1]
    front = mid_inv.shape[2]
    mid_rows = mid_inv.shape[1]
    nmiddle = mid_map.shape[0]
    root_order = root_inv.shape[1]
    root_rows = root_inv.shape[0]
    inv_block = mid_inv[0]
    cpl_block = mid_cpl[0]
    first_cols = col_id * share_rows + lax.iota(jnp.int32, share_rows)
    live = (first_cols[None, :] < leaf_size[:, None])[:, None, :]
    partial_value = jnp.einsum(
        "lkp,lpq->lkq", leaf_grad, leaf_inv, preferred_element_type=jnp.float32
    )
    leaf_y = jnp.where(
        live, lax.psum_scatter(partial_value, "col", scatter_dimension=2, tiled=True), 0.0
    )
    leaf_yb = leaf_y.astype(jnp.bfloat16)
    shares = jnp.einsum("lkp,lpc->klc", leaf_yb, leaf_cpl, preferred_element_type=jnp.float32)
    placed_cols = (
        leaf_map // mid_rows * ncolumns + leaf_parent[:, None]
    ) * mid_rows + leaf_map % mid_rows
    targets = placed_cols.reshape(-1)
    spread = (
        jnp.zeros((nrhs, nmiddle * front), jnp.float32).at[:, targets].add(shares.reshape(nrhs, -1))
    )
    arrived = lax.psum_scatter(spread, ("row", "col"), scatter_dimension=1, tiled=True)
    mid_hb = (mid_grad[:, 0, :].astype(jnp.float32) - arrived).astype(jnp.bfloat16)
    mid_part = jnp.dot(mid_hb, inv_block, preferred_element_type=jnp.float32)
    mid_y = lax.psum_scatter(mid_part, "row", scatter_dimension=1, tiled=True)
    mid_yb = mid_y.astype(jnp.bfloat16)
    mid_share = jnp.dot(mid_yb, cpl_block, preferred_element_type=jnp.float32)
    root_cols = lax.dynamic_index_in_dim(mid_map, col_id, 0, keepdims=False)
    root_term = jnp.zeros((nrhs, root_order), jnp.float32).at[:, root_cols].add(mid_share)
    root_total = lax.psum(root_term, ("row", "col"))
    root_slice = lax.dynamic_slice_in_dim(root_total, row_id * root_rows, root_rows, 1)
    root_hb = (root_grad.astype(jnp.float32) - root_slice).astype(jnp.bfloat16)
    root_y = lax.psum(jnp.dot(root_hb, root_inv, preferred_element_type=jnp.float32), "row")
    root_yb = root_y.astype(jnp.bfloat16)
    root_x = jnp.einsum("kq,pq->kp", root_yb, root_inv, preferred_element_type=jnp.float32)
    root_all = lax.all_gather(root_x.astype(jnp.bfloat16), "row", axis=1, tiled=True)
    coupled = root_all[:, root_cols]
    mid_wb = (
        mid_y - jnp.einsum("kc,bc->kb", coupled, cpl_block, preferred_element_type=jnp.float32)
    ).astype(jnp.bfloat16)
    full_w = lax.all_gather(mid_wb, "row", axis=1, tiled=True)
    mid_x = jnp.einsum("kq,bq->kb", full_w, inv_block, preferred_element_type=jnp.float32)
    all_mid = lax.all_gather(mid_x.astype(jnp.bfloat16), ("row", "col"), axis=1, tiled=True)
    picked = all_mid[:, targets].reshape(nrhs, nleaves, -1)
    leaf_w = leaf_y - jnp.einsum(
        "klc,lpc->lkp", picked, leaf_cpl, preferred_element_type=jnp.float32
    )
    leaf_wb = jnp.where(live, leaf_w, 0.0).astype(jnp.bfloat16)
    leaf_x = jnp.einsum(
        "lkq,lpq->lkp",
        lax.all_gather(leaf_wb, "col", axis=2, tiled=True),
        leaf_inv,
        preferred_element_type=jnp.float32,
    )
    return (leaf_x, mid_x[:, None, :], root_x)


def solution(mesh):
    placed = (
        P("row", None, "col"),
        P("row", "col", None),
        P("row", "col", None),
        P("row"),
        P("row"),
        P("row", None),
        P(None, "col", "row"),
        P("col", "row", None),
        P("col", "row", None),
        P(),
        P(None, "row"),
        P("row", None),
    )
    nrow, ncol = mesh.shape["row"], mesh.shape["col"]

    def run(*args):
        width = args[7].shape[1]
        kc, nleaf = args[0].shape[1] // ncol, args[0].shape[0]
        whole_tiles = width % LANES == 0 and kc % 8 == 0 and nleaf * kc % 32 == 0 and width * kc % 2048 == 0
        one_front = args[9].shape[0] == ncol and args[11].shape[0] == width
        if whole_tiles and one_front and nrow % 2 == 0 and nleaf % 2 == 0:
            return fused(nrow, ncol, *args)
        return body(*args)

    return jax.shard_map(
        run,
        mesh=mesh,
        in_specs=placed,
        out_specs=(P("row", None, "col"), P(None, "col", "row"), P(None, "row")),
        check_vma=False,
    )
```
